32 devices in a mesh: groups: 2 (over y), ctx: 2 (over x), exp: 8 (over z, core).
Axes of the slice: x: 2, y: 2, z: 4, core: 2. Of those that a mesh axis runs over, the one named last changes fastest.
Arguments:
- resid_in: bfloat16 [512, 3072], P(('groups', 'ctx', 'exp')), parts along dimension 0, may hold values from -6 to 6
- queries: bfloat16 [512, 2048], P(('groups', 'ctx'), 'exp'), parts along dimension 0, may hold values from -1.75 to 1.75
- keys: bfloat16 [512, 2048], P(('groups', 'ctx'), 'exp'), parts along dimension 0, may hold values from -1.75 to 1.75
- values: bfloat16 [512, 2048], P(('groups', 'ctx'), 'exp'), parts along dimension 0, may hold values from -40 to 40
- out_gate: bfloat16 [512, 2048], P(('groups', 'ctx'), 'exp'), parts along dimension 0, may hold values from -8 to 8
- log_decay: float32 [16, 512], P('exp', ('groups', 'ctx')), parts along dimension 1, may hold values from -1 to 0
- attn_gain: float32 [2048], P('exp'), may hold values from 0.1 to 1.9
- out_proj: bfloat16 [2048, 3072], P('exp'), may hold values from -0.125 to 0.125
- moe_gain: float32 [3072], replicated, may hold values from 0.1 to 1.9
- routes: int32 [512, 2], P(('groups', 'ctx', 'exp')), parts along dimension 0, may hold values from 0 to 3, all different within a row; in each aligned block of 16 rows (0 to 15, 16 to 31, ...) at most 12 rows name the same one
- route_weight: float32 [512, 2], P(('groups', 'ctx', 'exp')), parts along dimension 0, may hold values from 0.2 to 1
- w_gate: bfloat16 [8, 3072, 2304], P('exp', None, 'ctx'), may hold values from -0.109375 to 0.109375
- w_up: bfloat16 [8, 3072, 2304], P('exp', None, 'ctx'), may hold values from -0.109375 to 0.109375
- w_down: bfloat16 [8, 2304, 3072], P('exp', None, 'ctx'), may hold values from -0.09375 to 0.09375
Outputs:
- mixed: bfloat16 [512, 3072], P(('groups', 'ctx', 'exp')), parts along dimension 0
The draws below stay inside these ranges and needn't reach their ends.
There are 2 independent parts, one for each index of `groups`. The reference program is written for one: setup_inputs(seed, part) draws one part's arguments, and reference() takes and returns one part's arrays. A program takes and returns all parts, laid end to end along the dimension named above; an argument that names none is the same for every part. Nothing has to cross between parts.
Inputs may be any that keep to these rules, and one draw needn't show every extreme that they name: `routes`: each row names two different experts; in the 16 rows of one device no expert is named more than 12 times, and 12 is reached.
All inputs are finite; a program needn't handle non-finite values.
Results may differ from the reference program's by a relative error of at most 0.006.
Values may be sent and summed in bfloat16 or wider, within the bound.
A program may use at most 128 MiB of HBM per device.

```python
import math
import jax
import jax.numpy as jnp
import numpy as np
from jax import lax

D = 3072
HD = 128
FF = 4608
TOK_DEV = 128
HEAD_TOTAL = 16
WINDOW_TOKENS = 256
ROWS = 16
EXPERTS = 4
CAP = 12
N_CTX = 2


def draw_values(key, part):
    key = jax.random.fold_in(key, 5)
    first_key = jax.random.fold_in(key, 0)
    column_head = (jnp.arange(HEAD_TOTAL * HD, dtype=jnp.int32) // HD).astype(jnp.float32)
    level = column_head / max(HEAD_TOTAL - 1, 1)
    base_draw = jax.random.truncated_normal(first_key, -4.0, 4.0, (WINDOW_TOKENS, HEAD_TOTAL * HD), jnp.float32)
    scaled = base_draw * (10.0 ** (0.5 * level))[None, :]
    return scaled.astype(jnp.bfloat16)


def draw_log_decay(key, part):
    key = jax.random.fold_in(key, 11)
    every_key_row = jax.random.split(key, 6)
    fast_limit = 5
    fast_heads = jax.random.randint(every_key_row[0], (HEAD_TOTAL, 1), 0, 10) < fast_limit
    span = jax.random.uniform(every_key_row[1], (HEAD_TOTAL, 1), jnp.float32, 30.0, 50.0)
    keep_share = jax.random.uniform(every_key_row[2], (HEAD_TOTAL, 1), jnp.float32, 0.4, 0.8)
    jitter = jax.random.uniform(every_key_row[3], (HEAD_TOTAL, WINDOW_TOKENS), jnp.float32, 0.5, 1.5)
    base_rate = jnp.where(fast_heads, -1.0 / span, jnp.log(keep_share) / WINDOW_TOKENS)
    decay_rate_lookup = base_rate * jitter
    spike_position = jax.random.randint(every_key_row[4], (HEAD_TOTAL, 2), 0, WINDOW_TOKENS)
    token_offsets = jnp.arange(WINDOW_TOKENS, dtype=jnp.int32)
    spike_strike = jnp.any(token_offsets[None, :, None] == spike_position[:, None, :], axis=-1)
    spike_falloff = jnp.log(jax.random.uniform(every_key_row[5], (HEAD_TOTAL, WINDOW_TOKENS), jnp.float32, 0.6, 0.8))
    return jnp.where(spike_strike, decay_rate_lookup + spike_falloff, decay_rate_lookup)


def levels(rng, shape, shards, least, largest):
    level = 1.0
    for position, parts in shards:
        draws = jax.random.uniform(jax.random.fold_in(jax.random.fold_in(rng, 6), position), (parts,), jnp.float32, least / len(shards), largest / len(shards))
        level = level * jnp.repeat(jnp.exp(draws), shape[position] // parts).reshape((-1,) + (1,) * (len(shape) - 1 - position))
    return level


def deal_out(key, own, number, rows, amount, top, bound, skew):
    order = jax.random.permutation(key, amount)
    crowded, common = shares(amount, rows * top, bound, skew, True), shares(amount, rows * top, bound, skew, False)
    places = jnp.arange(amount)

    def named(lengths, offset_by):
        used = int((lengths > 0).sum())
        fixed = max(1, used // 4)
        passed = fixed + (places - fixed + offset_by * (used - fixed)) % max(1, amount - fixed)
        return jnp.zeros((amount,), jnp.int32).at[order[jnp.where(places < fixed, places, passed)]].set(jnp.asarray(lengths, jnp.int32))

    lengths = jnp.where(number % 4 == 0, named(crowded, number // 4), named(common, number - number // 4 - 1))
    mixed = jax.random.permutation(jax.random.fold_in(own, 3), amount)
    source_of, receiver = mixed[0:amount // 2 * 2:2], mixed[1:amount // 2 * 2:2]
    room = jnp.minimum(lengths[source_of] - 1, bound - lengths[receiver]) // 2
    room = jnp.where((source_of == order[0]) | (receiver == order[0]) | (lengths[receiver] == 0), 0, jnp.maximum(room, 0))
    passed = jax.random.randint(jax.random.fold_in(own, 4), (amount // 2,), 0, 1 << 20) % (room + 1)
    lengths = lengths.at[source_of].add(-passed).at[receiver].add(passed)
    labels = jnp.searchsorted(jnp.cumsum(lengths), jnp.arange(rows * top), side="right").astype(jnp.int32)
    listing = labels.reshape(top, rows).T
    listing = listing[jax.random.permutation(jax.random.fold_in(own, 1), rows)]
    offset_by = jax.random.randint(jax.random.fold_in(own, 2), (rows, 1), 0, top)
    return jnp.take_along_axis(listing, (jnp.arange(top)[None, :] + offset_by) % top, axis=1)


def shares(amount, total, reach, slope, full):
    loads = [(1 << 20) // math.isqrt(standing ** slope) + 1 for standing in range(1, amount + 1)]
    largest = reach if full else min(reach, max(-(-total // amount), total * loads[0] // sum(loads)))
    least = 1 if total - largest >= amount - 1 else 0
    given, rest = [largest] + [least] * (amount - 1), total - largest - least * (amount - 1)
    while rest > 0:
        movable = [i for i in range(1, amount) if given[i] < largest] or [i for i in range(1, amount) if given[i] < reach]
        pool, remaining = sum([loads[i] for i in movable]), rest
        for i in movable:
            addition = min(reach - given[i], max(1, remaining * loads[i] // pool), rest)
            given[i] = given[i] + addition
            rest = rest - addition
    return np.array(given)


def centred(own_key, extent, deviation, bound, cuts=(), kind=jnp.bfloat16):
    entries = deviation * jax.random.normal(own_key, extent, jnp.float32)
    if cuts:
        entries = entries * levels(own_key, extent, cuts, -0.22, 0.18)
    return jnp.clip(entries, -bound, bound).astype(kind)


def setup_inputs(seed: int = 0, part: int = 0) -> dict:
    seeds = jax.random.split(jax.random.key(seed), 15)
    part_splits = jax.random.split(jax.random.fold_in(seeds[14], part), 15)
    resid_in = centred(part_splits[0], (WINDOW_TOKENS, D), 1.0, 6.0, ((0, 16),))
    queries = centred(part_splits[1], (WINDOW_TOKENS, HEAD_TOTAL * HD), 0.3, 1.75, ((0, 2), (1, 8)))
    keys = centred(part_splits[2], (WINDOW_TOKENS, HEAD_TOTAL * HD), 0.3, 1.75, ((0, 2), (1, 8)))
    values = draw_values(jax.random.fold_in(jax.random.fold_in(seeds[14], part), 71), part)
    out_gate = centred(part_splits[4], (WINDOW_TOKENS, HEAD_TOTAL * HD), 1.5, 8.0, ((0, 2), (1, 8)))
    log_decay = draw_log_decay(jax.random.fold_in(jax.random.fold_in(seeds[14], part), 71), part)
    attn_gain = jnp.clip(1.0 + 0.18 * jax.random.normal(seeds[6], (HEAD_TOTAL * HD,), jnp.float32), 0.1, 1.9)
    out_proj = centred(seeds[7], (HEAD_TOTAL * HD, D), (HEAD_TOTAL * HD) ** -0.5, 0.125, ((0, 8),))
    moe_gain = jnp.clip(1.0 + 0.18 * jax.random.normal(seeds[8], (D,), jnp.float32), 0.1, 1.9)
    routes_keys = jax.random.split(jax.random.fold_in(part_splits[9], 1), WINDOW_TOKENS // ROWS)
    routes_turns = jax.random.permutation(jax.random.fold_in(part_splits[9], 3), WINDOW_TOKENS // ROWS)
    routes = jax.vmap(lambda own, number: deal_out(jax.random.fold_in(part_splits[9], 2), own, number, ROWS, EXPERTS, 2, CAP, 2))(routes_keys, routes_turns).reshape((WINDOW_TOKENS, 2))
    route_weight = jnp.clip(0.2 + 0.8 * jax.random.uniform(part_splits[10], (WINDOW_TOKENS, 2), jnp.float32) ** levels(part_splits[10], (WINDOW_TOKENS, 2), ((0, 16),), -0.2, 0.2), 0.2, 1.0)
    w_gate = centred(seeds[11], (2 * EXPERTS, D, FF // 2), D ** -0.5, 0.109375, ((0, 8), (2, 2)))
    w_up = centred(seeds[12], (2 * EXPERTS, D, FF // 2), D ** -0.5, 0.109375, ((0, 8), (2, 2)))
    w_down = centred(seeds[13], (2 * EXPERTS, FF // 2, D), FF ** -0.5, 0.09375, ((0, 8), (2, 2)))
    return {"resid_in": resid_in, "queries": queries, "keys": keys, "values": values, "out_gate": out_gate, "log_decay": log_decay, "attn_gain": attn_gain, "out_proj": out_proj, "moe_gain": moe_gain, "routes": routes, "route_weight": route_weight, "w_gate": w_gate, "w_up": w_up, "w_down": w_down}


HIGHEST = lax.Precision.HIGHEST

def local_terms(query_block, key_block, value_block, log_rates):
    cumulative = jnp.cumsum(log_rates, axis=1)
    scores = jnp.einsum('thd,shd->hts', query_block.astype(jnp.float32), key_block.astype(jnp.float32), precision=HIGHEST)
    length = log_rates.shape[1]
    later = jnp.arange(length, dtype=jnp.int32)[:, None] >= jnp.arange(length, dtype=jnp.int32)[None, :]
    spread = cumulative[:, :, None] - cumulative[:, None, :]
    weights = jnp.where(later[None], jnp.exp(jnp.minimum(spread, 0.0)), 0.0)
    value_float = value_block.astype(jnp.float32)
    inner_part = jnp.einsum('hts,shd->thd', scores * weights, value_float, precision=HIGHEST)
    tail_decay = jnp.exp(cumulative[:, -1:] - cumulative)
    key_scaled = key_block.astype(jnp.float32) * jnp.transpose(tail_decay)[:, :, None]
    local_state = jnp.einsum('shd,she->hde', key_scaled, value_float, precision=HIGHEST)
    query_scaled = query_block.astype(jnp.float32) * jnp.transpose(jnp.exp(cumulative))[:, :, None]
    return (inner_part, query_scaled, local_state, jnp.exp(cumulative[:, -1]))

def head_gate(attended, out_gate, attn_gain):
    token_count, head_count, head_width = attended.shape
    scale_rows = lax.rsqrt(lax.optimization_barrier(jnp.mean(attended * attended, axis=-1, keepdims=True)) + 1e-06)
    gain_table = attn_gain.reshape(head_count, head_width)
    opening = jax.nn.sigmoid(out_gate.astype(jnp.float32)).reshape(attended.shape)
    gated = opening * attended * scale_rows * gain_table
    return gated.reshape(token_count, head_count * head_width).astype(jnp.bfloat16)

def rms_rows(rows_in, gain):
    values_float = rows_in.astype(jnp.float32)
    scale_rows = lax.rsqrt(lax.optimization_barrier(jnp.mean(values_float * values_float, axis=-1, keepdims=True)) + 1e-06)
    return (values_float * scale_rows * gain).astype(jnp.bfloat16)

def slot_tables(route_rows, expert_count, capacity):
    leading = route_rows.shape[:-2]
    pair_ids = route_rows.reshape(leading + (-1,))
    onehot = (pair_ids[..., None] == jnp.arange(expert_count, dtype=jnp.int32)).astype(jnp.int32)
    earlier = jnp.cumsum(onehot, axis=-2) - onehot
    slot_ids = lax.optimization_barrier(jnp.sum(earlier * onehot, axis=-1))
    slot_hit = (slot_ids[..., None] == jnp.arange(capacity, dtype=jnp.int32)).astype(jnp.float32)
    expert_hit = onehot.astype(jnp.float32).reshape(route_rows.shape + (expert_count,))
    return (expert_hit, slot_hit.reshape(route_rows.shape + (capacity,)))

def reference(resid_in, queries, keys, values, out_gate, log_decay, attn_gain, out_proj, moe_gain, routes, route_weight, w_gate, w_up, w_down):
    head_shape = (N_CTX, TOK_DEV, HEAD_TOTAL, HD)
    blocks = (queries.reshape(head_shape), keys.reshape(head_shape), values.reshape(head_shape), jnp.transpose(log_decay.reshape(HEAD_TOTAL, N_CTX, TOK_DEV), (1, 0, 2)))

    def advance(state, pieces):
        inner_part, query_scaled, local_state, block_decay = local_terms(pieces[0], pieces[1], pieces[2], pieces[3])
        attended = inner_part + jnp.einsum('thd,hde->the', query_scaled, state, precision=HIGHEST)
        return (block_decay[:, None, None] * state + local_state, attended)
    start_state = jnp.zeros((HEAD_TOTAL, HD, HD), jnp.float32)
    _, attended = lax.scan(advance, start_state, blocks)
    attended = attended.reshape(WINDOW_TOKENS, HEAD_TOTAL, HD)
    gated = head_gate(attended, out_gate, attn_gain)
    attn_sum = jnp.dot(gated, out_proj, preferred_element_type=jnp.float32)
    resid = (resid_in.astype(jnp.float32) + attn_sum).astype(jnp.bfloat16)
    normed = rms_rows(resid, moe_gain)
    block_count = WINDOW_TOKENS // ROWS
    hit_expert, hit_slot = slot_tables(routes.reshape(block_count, ROWS, 2), EXPERTS, CAP)
    normed_blocks = normed.reshape(block_count, ROWS, D).astype(jnp.float32)
    weight_blocks = route_weight.reshape(block_count, ROWS, 2)
    gate_pairs = w_gate.reshape(EXPERTS, 2, D, FF // 2)
    up_pairs = w_up.reshape(EXPERTS, 2, D, FF // 2)
    down_pairs = w_down.reshape(EXPERTS, 2, FF // 2, D)

    def expert_step(running, expert):
        chosen = hit_expert[:, :, :, expert]
        picker = jnp.einsum('brk,brks->bsr', chosen, hit_slot)
        gathered = jnp.einsum('bsr,brd->bsd', picker, normed_blocks, precision=HIGHEST).astype(jnp.bfloat16)
        flat_rows = gathered.reshape(block_count * CAP, D)
        gate_full = jnp.concatenate([gate_pairs[expert, 0], gate_pairs[expert, 1]], axis=1)
        up_full = jnp.concatenate([up_pairs[expert, 0], up_pairs[expert, 1]], axis=1)
        down_full = jnp.concatenate([down_pairs[expert, 0], down_pairs[expert, 1]], axis=0)
        gate_part = jnp.dot(flat_rows, gate_full, preferred_element_type=jnp.float32)
        up_part = jnp.dot(flat_rows, up_full, preferred_element_type=jnp.float32)
        hidden = (jax.nn.silu(gate_part) * up_part).astype(jnp.bfloat16)
        expert_out = jnp.dot(hidden, down_full, preferred_element_type=jnp.float32).reshape(block_count, CAP, D)
        mixing = jnp.einsum('brk,brk,brks->brs', weight_blocks, chosen, hit_slot)
        return (running + jnp.einsum('brs,bsd->brd', mixing, expert_out, precision=HIGHEST), None)
    moe_sum, _ = lax.scan(expert_step, jnp.zeros((block_count, ROWS, D), jnp.float32), jnp.arange(EXPERTS, dtype=jnp.int32))
    return (resid.astype(jnp.float32) + moe_sum.reshape(WINDOW_TOKENS, D)).astype(jnp.bfloat16)
```

```python
import functools

import jax
import jax.numpy as jnp
from jax import lax
from jax.experimental import pallas as pl
from jax.experimental.pallas import tpu as pltpu
from jax.sharding import PartitionSpec as P

HIGHEST = lax.Precision.HIGHEST


def from_behind(block, axis, distance):
    devices = range(lax.axis_size(axis))
    route = [(i - distance, i) for i in devices if i - distance in devices]
    return lax.ppermute(block, axis, route)


def local_terms(query_block, key_block, value_block, log_rates):
    cumulative = jnp.cumsum(log_rates, axis=1)
    scores = jnp.einsum("thd,shd->hts", query_block, key_block, preferred_element_type=jnp.float32)
    length = log_rates.shape[1]
    later = (
        jnp.arange(length, dtype=jnp.int32)[:, None] >= jnp.arange(length, dtype=jnp.int32)[None, :]
    )
    spread = cumulative[:, :, None] - cumulative[:, None, :]
    weights = jnp.where(later[None], jnp.exp(jnp.minimum(spread, 0.0)), 0.0)
    value_float = value_block.astype(jnp.float32)
    inner_part = jnp.einsum("hts,shd->thd", scores * weights, value_float, precision=HIGHEST)
    tail_decay = jnp.exp(cumulative[:, -1:] - cumulative)
    key_scaled = key_block.astype(jnp.float32) * jnp.transpose(tail_decay)[:, :, None]
    local_state = jnp.einsum("shd,she->hde", key_scaled, value_float, precision=HIGHEST)
    query_scaled = query_block.astype(jnp.float32) * jnp.transpose(jnp.exp(cumulative))[:, :, None]
    return (inner_part, query_scaled, local_state, jnp.exp(cumulative[:, -1]))


def head_gate(attended, out_gate, attn_gain):
    token_count, head_count, head_width = attended.shape
    scale_rows = lax.rsqrt(jnp.mean(attended * attended, axis=-1, keepdims=True) + 1e-06)
    gain_table = attn_gain.reshape(head_count, head_width)
    opening = jax.nn.sigmoid(out_gate.astype(jnp.float32)).reshape(attended.shape)
    gated = opening * attended * scale_rows * gain_table
    return gated.reshape(token_count, head_count * head_width).astype(jnp.bfloat16)


def rms_rows(rows_in, gain):
    values_float = rows_in.astype(jnp.float32)
    scale_rows = lax.rsqrt(jnp.mean(values_float * values_float, axis=-1, keepdims=True) + 1e-06)
    return (values_float * scale_rows * gain).astype(jnp.bfloat16)


def slot_tables(route_rows, expert_count, capacity):
    leading = route_rows.shape[:-2]
    pair_ids = route_rows.reshape(leading + (-1,))
    onehot = (pair_ids[..., None] == jnp.arange(expert_count, dtype=jnp.int32)).astype(jnp.int32)
    earlier = jnp.cumsum(onehot, axis=-2) - onehot
    slot_ids = jnp.sum(earlier * onehot, axis=-1)
    slot_hit = (slot_ids[..., None] == jnp.arange(capacity, dtype=jnp.int32)).astype(jnp.float32)
    expert_hit = onehot.astype(jnp.float32).reshape(route_rows.shape + (expert_count,))
    return (expert_hit, slot_hit.reshape(route_rows.shape + (capacity,)))


def per_device(
    resid_in,
    queries,
    keys,
    values,
    out_gate,
    log_decay,
    attn_gain,
    out_proj,
    moe_gain,
    routes,
    route_weight,
    w_gate,
    w_up,
    w_down,
):
    head_count = log_decay.shape[0]
    token_count = queries.shape[0]
    head_width = queries.shape[1] // head_count
    shaped = (token_count, head_count, head_width)
    inner_part, query_scaled, local_state, block_decay = local_terms(
        queries.reshape(shaped), keys.reshape(shaped), values.reshape(shaped), log_decay
    )
    ctx_size = lax.axis_size("ctx")
    exp_size = lax.axis_size("exp")
    empty_state = jnp.zeros_like(local_state)

    def advance(turn_index, incoming):
        carried = block_decay[:, None, None] * incoming + local_state
        return from_behind(carried, "ctx", 1)

    incoming = lax.fori_loop(0, ctx_size - 1, advance, empty_state)
    attended = inner_part + jnp.einsum("thd,hde->the", query_scaled, incoming, precision=HIGHEST)
    gated = head_gate(attended, out_gate, attn_gain)
    attn_sum = lax.psum_scatter(
        jnp.dot(gated, out_proj, preferred_element_type=jnp.float32),
        "exp",
        scatter_dimension=0,
        tiled=True,
    )
    resid = (resid_in.astype(jnp.float32) + attn_sum).astype(jnp.bfloat16)
    normed = rms_rows(resid, moe_gain)
    row_count = resid.shape[0]
    expert_count = exp_size // 2
    capacity = min(row_count, 6 * token_count // (exp_size * exp_size))
    hit_expert, hit_slot = slot_tables(routes, expert_count, capacity)
    gate_local = w_gate[0]
    up_local = w_up[0]
    down_local = w_down[0]
    all_rows, all_routes = (
        lax.all_gather(normed[None], "ctx", axis=0, tiled=True),
        lax.all_gather(routes[None], "ctx", axis=0, tiled=True),
    )
    every_expert, every_slot = slot_tables(all_routes, expert_count, capacity)
    picker = jnp.repeat(jnp.einsum("crke,crks->cesr", every_expert, every_slot), 2, axis=1).astype(
        jnp.bfloat16
    )
    outgoing = jnp.einsum(
        "cosr,crd->cosd", picker, all_rows, preferred_element_type=jnp.float32
    ).astype(jnp.bfloat16)
    arrived = lax.all_to_all(outgoing, "exp", split_axis=1, concat_axis=1, tiled=True)
    gate_part = jnp.einsum("abcd,dh->abch", arrived, gate_local, preferred_element_type=jnp.float32)
    up_part = jnp.einsum("abcd,dh->abch", arrived, up_local, preferred_element_type=jnp.float32)
    hidden = (jax.nn.silu(gate_part) * up_part).astype(jnp.bfloat16)
    partial_out = jnp.einsum(
        "abch,hn->abcn",
        lax.all_gather(hidden, "ctx", axis=3, tiled=True),
        down_local,
        preferred_element_type=jnp.float32,
    )
    came_back = lax.all_to_all(
        lax.all_to_all(partial_out, "ctx", split_axis=0, concat_axis=3, tiled=True),
        "exp",
        split_axis=1,
        concat_axis=1,
        tiled=True,
    )
    halves = came_back[0].reshape(expert_count, 2, capacity, came_back.shape[-1])
    paired = halves[:, 0] + halves[:, 1]
    mixing = jnp.einsum("rk,rke,rks->res", route_weight, hit_expert, hit_slot)
    moe_sum = jnp.einsum("res,esd->rd", mixing, paired, precision=HIGHEST)
    return (resid.astype(jnp.float32) + moe_sum).astype(jnp.bfloat16)


MESH = pl.DeviceIdType.MESH
PROJ_TILES = 3
WIDE = 256


def dot32(left, right):
    return jnp.dot(left, right, preferred_element_type=jnp.float32)


def layer_kernel(
    zs,
    capacity,
    resid_in,
    queries,
    keys,
    values,
    out_gate,
    log_decay,
    attn_gain,
    out_proj_hbm,
    moe_gain,
    routes,
    route_weight,
    w_gate_hbm,
    w_up_hbm,
    w_down_hbm,
    mixed,
    out_proj,
    w_gate,
    w_up,
    w_rest,
    w_down,
    info,
    state_out,
    state_in,
    gated,
    pair_out,
    pair_in,
    proj_out,
    proj_in,
    resid,
    rows_in,
    picked,
    hidden_own,
    hidden_in,
    expert_sum,
    half_out,
    half_in,
    back_out,
    back_in,
    last_out,
    last_in,
    load_sem,
    info_send,
    info_recv,
    one_send,
    one_recv,
    pair_send,
    pair_recv,
    proj_send,
    proj_recv,
    gather_send,
    gather_recv,
    hidden_send,
    hidden_recv,
    half_send,
    half_recv,
    back_send,
    back_recv,
):
    ctx = lax.axis_index("ctx")
    exp = lax.axis_index("exp")
    core = lax.rem(exp, 2)
    level = exp // 2
    row_count, width = resid_in.shape
    tokens = queries.shape[0]
    heads = log_decay.shape[0]
    head_width = queries.shape[1] // heads
    half = w_gate_hbm.shape[2]
    whole = half // WIDE * WIDE
    rest = half - whole
    columns = w_down_hbm.shape[2]
    cap_rows = zs * capacity
    tile = width // PROJ_TILES
    other_ctx = 1 - ctx

    def ahead(d):
        return lax.rem(level + d, zs)

    def behind(d):
        return lax.rem(level + zs - d, zs)

    def device(at_ctx, at_level, at_core):
        return {"ctx": at_ctx, "exp": at_level * 2 + at_core}

    core_partner = device(ctx, level, 1 - core)
    ctx_partner = device(other_ctx, level, core)

    loads = [
        pltpu.make_async_copy(out_proj_hbm, out_proj, load_sem.at[0]),
        pltpu.make_async_copy(w_gate_hbm.at[0, :, pl.ds(0, whole)], w_gate, load_sem.at[1]),
        pltpu.make_async_copy(w_up_hbm.at[0, :, pl.ds(0, whole)], w_up, load_sem.at[2]),
        pltpu.make_async_copy(
            w_gate_hbm.at[0, :, pl.ds(whole, rest)], w_rest.at[:, pl.ds(0, rest)], load_sem.at[3]
        ),
        pltpu.make_async_copy(
            w_up_hbm.at[0, :, pl.ds(whole, rest)], w_rest.at[:, pl.ds(rest, rest)], load_sem.at[4]
        ),
        pltpu.make_async_copy(w_down_hbm.at[0], w_down, load_sem.at[5]),
    ]
    for load in loads:
        load.start()

    barrier = pltpu.get_barrier_semaphore()
    peers = [core_partner, ctx_partner]
    for d in range(1, zs):
        peers.append(device(ctx, ahead(d), core))
        peers.append(device(other_ctx, ahead(d), core))
    for peer in peers:
        pl.semaphore_signal(barrier, inc=1, device_id=peer, device_id_type=MESH)

    def send(source, target, send_sem, recv_sem, peer):
        copy = pltpu.make_async_remote_copy(
            src_ref=source,
            dst_ref=target,
            send_sem=send_sem,
            recv_sem=recv_sem,
            device_id=peer,
            device_id_type=MESH,
        )
        copy.start()
        return copy

    sent = []
    lane = lax.broadcasted_iota(jnp.int32, (row_count, 128), 1)
    own_routes = routes[...].astype(jnp.float32)
    own_weight = route_weight[...]
    info[0, 0] = jnp.where(
        lane == 0,
        own_routes[:, 0:1],
        jnp.where(
            lane == 1,
            own_routes[:, 1:2],
            jnp.where(lane == 2, own_weight[:, 0:1], own_weight[:, 1:2]),
        ),
    )

    later_row = lax.broadcasted_iota(jnp.int32, (tokens, tokens), 0)
    later_col = lax.broadcasted_iota(jnp.int32, (tokens, tokens), 1)
    causal = later_row >= later_col
    sums = []
    for h in range(heads):
        span = pl.ds(h * head_width, head_width)
        spread = jnp.broadcast_to(log_decay[h : h + 1, :], (tokens, tokens))
        upright = jnp.transpose(spread)
        cum_col = jnp.sum(jnp.where(causal, spread, 0.0), axis=1, keepdims=True)
        cum_row = jnp.sum(jnp.where(later_row <= later_col, upright, 0.0), axis=0, keepdims=True)
        sums.append((cum_col, cum_row))
        tail = jnp.exp(cum_row[:, tokens - 1 : tokens] - cum_row)
        key_up = jnp.transpose(keys[:, span].astype(jnp.float32)) * tail
        state_out[h] = dot32(key_up.astype(jnp.bfloat16), values[:, span]).astype(jnp.bfloat16)

    pl.semaphore_wait(barrier, len(peers))
    state_copy = send(state_out, state_in, one_send.at[0], one_recv.at[0], ctx_partner)
    infos = []
    for rel in range(2):
        for d in range(zs):
            if rel or d:
                infos.append(
                    send(
                        info.at[0, 0],
                        info.at[rel, d],
                        info_send.at[rel * zs + d],
                        info_recv.at[rel * zs + d],
                        device(other_ctx if rel else ctx, ahead(d), core),
                    )
                )
    inner = []
    for h in range(heads):
        span = pl.ds(h * head_width, head_width)
        cum_col, cum_row = sums[h]
        scores = lax.dot_general(
            queries[:, span],
            keys[:, span],
            (((1,), (1,)), ((), ())),
            preferred_element_type=jnp.float32,
        )
        decay = jnp.where(causal, jnp.exp(jnp.minimum(cum_col - cum_row, 0.0)), 0.0)
        inner.append(dot32((scores * decay).astype(jnp.bfloat16), values[:, span]))
    state_copy.wait_recv()
    for h in range(heads):
        span = pl.ds(h * head_width, head_width)
        earlier = dot32(queries[:, span], state_in[h]) * jnp.exp(sums[h][0])
        attended = inner[h] + jnp.where(ctx == 0, 0.0, earlier)
        scale = lax.rsqrt(jnp.mean(attended * attended, axis=-1, keepdims=True) + 1e-06)
        opening = jax.nn.sigmoid(out_gate[:, span].astype(jnp.float32))
        gated[:, span] = (opening * attended * scale * attn_gain[:, span]).astype(jnp.bfloat16)

    order = [
        gated[pl.ds(pl.multiple_of(2 * row_count * ahead(d) + row_count * side, row_count), row_count), :]
        for side in (1 - core, core)
        for d in range(zs)
    ]
    ordered = jnp.concatenate(order, axis=0)
    loads[0].wait()
    split = zs * row_count
    pairs = []
    mine = []
    for n in range(PROJ_TILES):
        product = dot32(ordered, out_proj[:, n * tile : (n + 1) * tile])
        pair_out[n] = product[:split].astype(jnp.bfloat16)
        pairs.append(send(pair_out.at[n], pair_in.at[n], pair_send.at[n], pair_recv.at[n], core_partner))
        mine.append(product[split:])
    projected = []
    for n in range(PROJ_TILES):
        pairs[n].wait_recv()
        total = mine[n] + pair_in[n].astype(jnp.float32)
        for d in range(1, zs):
            proj_out[n, d] = total[d * row_count : (d + 1) * row_count].astype(jnp.bfloat16)
            projected.append(
                send(
                    proj_out.at[n, d],
                    proj_in.at[n, d],
                    proj_send.at[n * zs + d],
                    proj_recv.at[n * zs + d],
                    device(ctx, ahead(d), core),
                )
            )
        part = slice(n * tile, (n + 1) * tile)
        resid[:, part] = resid_in[:, part].astype(jnp.float32) + total[:row_count]

    for copy in infos:
        copy.wait_recv()
    block = row_count
    routed = info[...].reshape(2 * zs * block, 128)
    routed_up = jnp.transpose(routed)
    mark = level.astype(jnp.float32)
    count = 2 * zs * block
    place_row = lax.broadcasted_iota(jnp.int32, (count, count), 0)
    place_col = lax.broadcasted_iota(jnp.int32, (count, count), 1)
    same = place_row // block == place_col // block
    hit_col = jnp.where((routed[:, 0:1] == mark) | (routed[:, 1:2] == mark), 1.0, 0.0)
    hit_row = jnp.where((routed_up[0:1] == mark) | (routed_up[1:2] == mark), 1.0, 0.0)
    slot_row = jnp.sum(
        jnp.where(same & (place_row < place_col), hit_col, 0.0), axis=0, keepdims=True
    ).astype(jnp.int32)
    slot_col = jnp.sum(
        jnp.where(same & (place_col < place_row), hit_row, 0.0), axis=1, keepdims=True
    ).astype(jnp.int32)
    index_row = lax.broadcasted_iota(jnp.int32, (1, count), 1) // block * capacity + slot_row
    index_col = lax.broadcasted_iota(jnp.int32, (count, 1), 0) // block * capacity + slot_col
    reach_rows = lax.broadcasted_iota(jnp.int32, (cap_rows, count), 0)
    picker = jnp.where((reach_rows == index_row) & (hit_row > 0.5), 1.0, 0.0).astype(jnp.bfloat16)
    reach_cols = lax.broadcasted_iota(jnp.int32, (count, 2 * cap_rows), 1)
    placer = jnp.where((reach_cols == index_col) & (hit_col > 0.5), 1.0, 0.0).astype(jnp.bfloat16)

    for n in range(PROJ_TILES):
        part = slice(n * tile, (n + 1) * tile)
        for d in range(1, zs):
            projected[n * (zs - 1) + d - 1].wait_recv()
            resid[:, part] += proj_in[n, d].astype(jnp.float32)
    settled = resid[...].astype(jnp.bfloat16).astype(jnp.float32)
    resid[...] = settled
    scale = lax.rsqrt(jnp.mean(settled * settled, axis=-1, keepdims=True) + 1e-06)
    rows_in[0] = (settled * scale * moe_gain[...]).astype(jnp.bfloat16)
    gathers = [
        send(
            rows_in.at[0],
            rows_in.at[d],
            gather_send.at[d],
            gather_recv.at[d],
            device(ctx, ahead(d), core),
        )
        for d in range(1, zs)
    ]
    for copy in gathers:
        copy.wait_recv()
    picked[0, 0] = dot32(
        picker[:, : zs * block], rows_in[...].reshape(zs * block, width)
    ).astype(jnp.bfloat16)
    to_ctx = send(picked.at[0, 0], picked.at[1, 0], one_send.at[1], one_recv.at[1], ctx_partner)
    to_core = send(picked.at[0, 0], picked.at[0, 1], one_send.at[2], one_recv.at[2], core_partner)
    sent += [to_ctx, to_core]
    to_core.wait_recv()

    def activate(gate_part, up_part):
        return (jax.nn.silu(gate_part) * up_part).astype(jnp.bfloat16)

    def hide(rel):
        def step(n, carry):
            span = pl.ds(pl.multiple_of(n * WIDE, WIDE), WIDE)
            rows = picked[rel].reshape(2 * cap_rows, width)
            hidden_own[rel, :, span] = activate(
                dot32(rows, w_gate[:, span]), dot32(rows, w_up[:, span])
            )
            return carry

        lax.fori_loop(0, whole // WIDE, step, 0)
        both = dot32(picked[rel].reshape(2 * cap_rows, width), w_rest[...])
        hidden_own[rel, :, whole:] = activate(both[:, :rest], both[:, rest:])
        return send(
            hidden_own.at[rel],
            hidden_in.at[1 - rel],
            hidden_send.at[rel],
            hidden_recv.at[1 - rel],
            ctx_partner,
        )

    def lower(rel, first):
        source = hidden_own if first else hidden_in
        side = ctx if first else other_ctx

        def step(n, carry):
            span = pl.ds(pl.multiple_of(n * WIDE, WIDE), WIDE)
            product = dot32(
                source[rel], w_down[pl.ds(pl.multiple_of(side * half, 128), half), span]
            )
            if first:
                expert_sum[rel, :, span] = product
            else:
                expert_sum[rel, :, span] += product
            return carry

        lax.fori_loop(0, columns // WIDE, step, 0)

    for load in loads[1:5]:
        load.wait()
    hidden_near = hide(0)
    to_ctx.wait_recv()
    passed = send(picked.at[1, 0], picked.at[1, 1], one_send.at[3], one_recv.at[3], core_partner)
    passed.wait_recv()
    hidden_far = hide(1)
    loads[5].wait()
    lower(0, True)
    lower(1, True)

    def incoming_hidden(rel):
        return pltpu.make_async_remote_copy(
            src_ref=hidden_own.at[1 - rel],
            dst_ref=hidden_in.at[rel],
            send_sem=hidden_send.at[1 - rel],
            recv_sem=hidden_recv.at[rel],
            device_id=ctx_partner,
            device_id_type=MESH,
        )

    halves = [None, None]
    for rel in (1, 0):
        incoming_hidden(rel).wait_recv()
        lower(rel, False)
        half_out[rel] = expert_sum[rel, cap_rows:, :].astype(jnp.bfloat16)
        halves[rel] = send(
            half_out.at[rel], half_in.at[rel], half_send.at[rel], half_recv.at[rel], core_partner
        )
    backs = {}
    for rel in (1, 0):
        halves[rel].wait_recv()
        total = (expert_sum[rel, :cap_rows, :] + half_in[rel].astype(jnp.float32)).astype(jnp.bfloat16)
        chosen = placer[rel * zs * block : (rel + 1) * zs * block, rel * cap_rows : (rel + 1) * cap_rows]
        spread_rows = dot32(chosen, total).astype(jnp.bfloat16)
        back_in[rel, 0] = spread_rows[:block]
        for d in range(1, zs):
            back_out[rel, d] = spread_rows[d * block : (d + 1) * block]
            backs[rel, d] = send(
                back_out.at[rel, d],
                back_in.at[rel, d],
                back_send.at[rel * zs + d],
                back_recv.at[rel * zs + d],
                device(ctx, behind(d), core),
            )

    def mix(rel):
        table = info[rel, 0]
        total = jnp.zeros((block, columns), jnp.float32)
        for d in range(zs):
            if d:
                backs[rel, d].wait_recv()
            expert = ahead(d).astype(jnp.float32)
            weight = jnp.where(table[:, 0:1] == expert, table[:, 2:3], 0.0) + jnp.where(
                table[:, 1:2] == expert, table[:, 3:4], 0.0
            )
            total = total + weight * back_in[rel, d].astype(jnp.float32)
        return total

    last_out[...] = mix(1).astype(jnp.bfloat16)
    last = send(last_out, last_in, one_send.at[4], one_recv.at[4], ctx_partner)
    near = pl.ds(pl.multiple_of(ctx * columns, 128), columns)
    far = pl.ds(pl.multiple_of(other_ctx * columns, 128), columns)
    mixed[:, near] = (resid[:, near] + mix(0)).astype(jnp.bfloat16)
    last.wait_recv()
    mixed[:, far] = (resid[:, far] + last_in[...].astype(jnp.float32)).astype(jnp.bfloat16)

    sent += [state_copy, hidden_near, hidden_far, passed, last]
    for copy in sent + infos + pairs + projected + gathers + halves + list(backs.values()):
        copy.wait_send()


def per_device_kernel(
    resid_in,
    queries,
    keys,
    values,
    out_gate,
    log_decay,
    attn_gain,
    out_proj,
    moe_gain,
    routes,
    route_weight,
    w_gate,
    w_up,
    w_down,
):
    zs = lax.axis_size("exp") // 2
    row_count, width = resid_in.shape
    tokens = queries.shape[0]
    heads = log_decay.shape[0]
    head_width = queries.shape[1] // heads
    capacity = min(row_count, 6 * tokens // (4 * zs * zs))
    cap_rows = zs * capacity
    half = w_gate.shape[2]
    whole = half // WIDE * WIDE
    rest = half - whole
    columns = w_down.shape[2]
    tile = width // PROJ_TILES
    low = jnp.bfloat16
    dma = pltpu.SemaphoreType.DMA
    vmem = pl.BlockSpec(memory_space=pltpu.VMEM)
    away = pl.BlockSpec(memory_space=pl.ANY)
    return pl.pallas_call(
        functools.partial(layer_kernel, zs, capacity),
        out_shape=jax.ShapeDtypeStruct((row_count, width), low),
        in_specs=[vmem] * 7 + [away] + [vmem] * 3 + [away] * 3,
        out_specs=vmem,
        scratch_shapes=[
            pltpu.VMEM(out_proj.shape, low),
            pltpu.VMEM((width, whole), low),
            pltpu.VMEM((width, whole), low),
            pltpu.VMEM((width, 2 * rest), low),
            pltpu.VMEM(w_down.shape[1:], low),
            pltpu.VMEM((2, zs, row_count, 128), jnp.float32),
            pltpu.VMEM((heads, head_width, head_width), low),
            pltpu.VMEM((heads, head_width, head_width), low),
            pltpu.VMEM(queries.shape, low),
            pltpu.VMEM((PROJ_TILES, zs * row_count, tile), low),
            pltpu.VMEM((PROJ_TILES, zs * row_count, tile), low),
            pltpu.VMEM((PROJ_TILES, zs, row_count, tile), low),
            pltpu.VMEM((PROJ_TILES, zs, row_count, tile), low),
            pltpu.VMEM((row_count, width), jnp.float32),
            pltpu.VMEM((zs, row_count, width), low),
            pltpu.VMEM((2, 2, cap_rows, width), low),
            pltpu.VMEM((2, 2 * cap_rows, half), low),
            pltpu.VMEM((2, 2 * cap_rows, half), low),
            pltpu.VMEM((2, 2 * cap_rows, columns), jnp.float32),
            pltpu.VMEM((2, cap_rows, columns), low),
            pltpu.VMEM((2, cap_rows, columns), low),
            pltpu.VMEM((2, zs, row_count, columns), low),
            pltpu.VMEM((2, zs, row_count, columns), low),
            pltpu.VMEM((row_count, columns), low),
            pltpu.VMEM((row_count, columns), low),
            dma((6,)),
            dma((2 * zs,)),
            dma((2 * zs,)),
            dma((5,)),
            dma((5,)),
            dma((PROJ_TILES,)),
            dma((PROJ_TILES,)),
            dma((PROJ_TILES * zs,)),
            dma((PROJ_TILES * zs,)),
            dma((zs,)),
            dma((zs,)),
            dma((2,)),
            dma((2,)),
            dma((2,)),
            dma((2,)),
            dma((2 * zs,)),
            dma((2 * zs,)),
        ],
        compiler_params=pltpu.CompilerParams(
            collective_id=0, has_side_effects=True, vmem_limit_bytes=56 * 1024 * 1024
        ),
        cost_estimate=pl.CostEstimate(
            flops=12 * cap_rows * width * half * 2, bytes_accessed=6 * width * half, transcendentals=0
        ),
    )(
        resid_in,
        queries,
        keys,
        values,
        out_gate,
        log_decay,
        attn_gain.reshape(1, -1),
        out_proj,
        moe_gain.reshape(1, -1),
        routes,
        route_weight,
        w_gate,
        w_up,
        w_down,
    )


def solution(mesh):
    pairs_of_two = mesh.shape["ctx"] == 2 and mesh.shape["exp"] % 2 == 0
    return jax.shard_map(
        per_device_kernel if pairs_of_two else per_device,
        mesh=mesh,
        in_specs=(
            P(("groups", "ctx", "exp"), None),
            P(("groups", "ctx"), "exp"),
            P(("groups", "ctx"), "exp"),
            P(("groups", "ctx"), "exp"),
            P(("groups", "ctx"), "exp"),
            P("exp", ("groups", "ctx")),
            P("exp"),
            P("exp", None),
            P(),
            P(("groups", "ctx", "exp"), None),
            P(("groups", "ctx", "exp"), None),
            P("exp", None, "ctx"),
            P("exp", None, "ctx"),
            P("exp", None, "ctx"),
        ),
        out_specs=P(("groups", "ctx", "exp"), None),
        check_vma=False,
    )
```

```python
import functools

import jax
import jax.numpy as jnp
from jax import lax
from jax.experimental import pallas as pl
from jax.experimental.pallas import tpu as pltpu
from jax.sharding import PartitionSpec as P

HIGHEST = lax.Precision.HIGHEST


def from_behind(block, axis, distance):
    devices = range(lax.axis_size(axis))
    route = [(i - distance, i) for i in devices if i - distance in devices]
    return lax.ppermute(block, axis, route)


def local_terms(query_block, key_block, value_block, log_rates):
    cumulative = jnp.cumsum(log_rates, axis=1)
    scores = jnp.einsum("thd,shd->hts", query_block, key_block, preferred_element_type=jnp.float32)
    length = log_rates.shape[1]
    later = (
        jnp.arange(length, dtype=jnp.int32)[:, None] >= jnp.arange(length, dtype=jnp.int32)[None, :]
    )
    spread = cumulative[:, :, None] - cumulative[:, None, :]
    weights = jnp.where(later[None], jnp.exp(jnp.minimum(spread, 0.0)), 0.0)
    value_float = value_block.astype(jnp.float32)
    inner_part = jnp.einsum("hts,shd->thd", scores * weights, value_float, precision=HIGHEST)
    tail_decay = jnp.exp(cumulative[:, -1:] - cumulative)
    key_scaled = key_block.astype(jnp.float32) * jnp.transpose(tail_decay)[:, :, None]
    local_state = jnp.einsum("shd,she->hde", key_scaled, value_float, precision=HIGHEST)
    query_scaled = query_block.astype(jnp.float32) * jnp.transpose(jnp.exp(cumulative))[:, :, None]
    return (inner_part, query_scaled, local_state, jnp.exp(cumulative[:, -1]))


def head_gate(attended, out_gate, attn_gain):
    token_count, head_count, head_width = attended.shape
    scale_rows = lax.rsqrt(jnp.mean(attended * attended, axis=-1, keepdims=True) + 1e-06)
    gain_table = attn_gain.reshape(head_count, head_width)
    opening = jax.nn.sigmoid(out_gate.astype(jnp.float32)).reshape(attended.shape)
    gated = opening * attended * scale_rows * gain_table
    return gated.reshape(token_count, head_count * head_width).astype(jnp.bfloat16)


def rms_rows(rows_in, gain):
    values_float = rows_in.astype(jnp.float32)
    scale_rows = lax.rsqrt(jnp.mean(values_float * values_float, axis=-1, keepdims=True) + 1e-06)
    return (values_float * scale_rows * gain).astype(jnp.bfloat16)


def slot_tables(route_rows, expert_count, capacity):
    leading = route_rows.shape[:-2]
    pair_ids = route_rows.reshape(leading + (-1,))
    onehot = (pair_ids[..., None] == jnp.arange(expert_count, dtype=jnp.int32)).astype(jnp.int32)
    earlier = jnp.cumsum(onehot, axis=-2) - onehot
    slot_ids = jnp.sum(earlier * onehot, axis=-1)
    slot_hit = (slot_ids[..., None] == jnp.arange(capacity, dtype=jnp.int32)).astype(jnp.float32)
    expert_hit = onehot.astype(jnp.float32).reshape(route_rows.shape + (expert_count,))
    return (expert_hit, slot_hit.reshape(route_rows.shape + (capacity,)))


def per_device(
    resid_in,
    queries,
    keys,
    values,
    out_gate,
    log_decay,
    attn_gain,
    out_proj,
    moe_gain,
    routes,
    route_weight,
    w_gate,
    w_up,
    w_down,
):
    head_count = log_decay.shape[0]
    token_count = queries.shape[0]
    head_width = queries.shape[1] // head_count
    shaped = (token_count, head_count, head_width)
    inner_part, query_scaled, local_state, block_decay = local_terms(
        queries.reshape(shaped), keys.reshape(shaped), values.reshape(shaped), log_decay
    )
    ctx_size = lax.axis_size("ctx")
    exp_size = lax.axis_size("exp")
    empty_state = jnp.zeros_like(local_state)

    def advance(turn_index, incoming):
        carried = block_decay[:, None, None] * incoming + local_state
        return from_behind(carried, "ctx", 1)

    incoming = lax.fori_loop(0, ctx_size - 1, advance, empty_state)
    attended = inner_part + jnp.einsum("thd,hde->the", query_scaled, incoming, precision=HIGHEST)
    gated = head_gate(attended, out_gate, attn_gain)
    attn_sum = lax.psum_scatter(
        jnp.dot(gated, out_proj, preferred_element_type=jnp.float32),
        "exp",
        scatter_dimension=0,
        tiled=True,
    )
    resid = (resid_in.astype(jnp.float32) + attn_sum).astype(jnp.bfloat16)
    normed = rms_rows(resid, moe_gain)
    row_count = resid.shape[0]
    expert_count = exp_size // 2
    capacity = min(row_count, 6 * token_count // (exp_size * exp_size))
    hit_expert, hit_slot = slot_tables(routes, expert_count, capacity)
    gate_local = w_gate[0]
    up_local = w_up[0]
    down_local = w_down[0]
    all_rows, all_routes = (
        lax.all_gather(normed[None], "ctx", axis=0, tiled=True),
        lax.all_gather(routes[None], "ctx", axis=0, tiled=True),
    )
    every_expert, every_slot = slot_tables(all_routes, expert_count, capacity)
    picker = jnp.repeat(jnp.einsum("crke,crks->cesr", every_expert, every_slot), 2, axis=1).astype(
        jnp.bfloat16
    )
    outgoing = jnp.einsum(
        "cosr,crd->cosd", picker, all_rows, preferred_element_type=jnp.float32
    ).astype(jnp.bfloat16)
    arrived = lax.all_to_all(outgoing, "exp", split_axis=1, concat_axis=1, tiled=True)
    gate_part = jnp.einsum("abcd,dh->abch", arrived, gate_local, preferred_element_type=jnp.float32)
    up_part = jnp.einsum("abcd,dh->abch", arrived, up_local, preferred_element_type=jnp.float32)
    hidden = (jax.nn.silu(gate_part) * up_part).astype(jnp.bfloat16)
    partial_out = jnp.einsum(
        "abch,hn->abcn",
        lax.all_gather(hidden, "ctx", axis=3, tiled=True),
        down_local,
        preferred_element_type=jnp.float32,
    )
    came_back = lax.all_to_all(
        lax.all_to_all(partial_out, "ctx", split_axis=0, concat_axis=3, tiled=True),
        "exp",
        split_axis=1,
        concat_axis=1,
        tiled=True,
    )
    halves = came_back[0].reshape(expert_count, 2, capacity, came_back.shape[-1])
    paired = halves[:, 0] + halves[:, 1]
    mixing = jnp.einsum("rk,rke,rks->res", route_weight, hit_expert, hit_slot)
    moe_sum = jnp.einsum("res,esd->rd", mixing, paired, precision=HIGHEST)
    return (resid.astype(jnp.float32) + moe_sum).astype(jnp.bfloat16)


MESH = pl.DeviceIdType.MESH
PROJ_TILES = 3
WIDE = 256


def dot32(left, right):
    return jnp.dot(left, right, preferred_element_type=jnp.float32)


def layer_kernel(
    zs,
    capacity,
    resid_in,
    queries,
    keys,
    values,
    out_gate,
    log_decay,
    attn_gain,
    out_proj_hbm,
    moe_gain,
    routes,
    route_weight,
    w_gate_hbm,
    w_up_hbm,
    w_down_hbm,
    mixed,
    out_proj,
    w_gate,
    w_up,
    w_rest,
    w_down,
    info,
    state_out,
    state_in,
    gated,
    pair_out,
    pair_in,
    proj_out,
    proj_in,
    resid,
    rows_in,
    picked,
    hidden_own,
    hidden_in,
    expert_sum,
    half_out,
    half_in,
    back_out,
    back_in,
    last_out,
    last_in,
    load_sem,
    info_send,
    info_recv,
    one_send,
    one_recv,
    pair_send,
    pair_recv,
    proj_send,
    proj_recv,
    gather_send,
    gather_recv,
    ctx_send,
    ctx_recv,
    core_send,
    core_recv,
    pass_send,
    pass_recv,
    hidden_send,
    hidden_recv,
    half_send,
    half_recv,
    back_send,
    back_recv,
):
    ctx = lax.axis_index("ctx")
    exp = lax.axis_index("exp")
    core = lax.rem(exp, 2)
    level = exp // 2
    row_count, width = resid_in.shape
    tokens = queries.shape[0]
    heads = log_decay.shape[0]
    head_width = queries.shape[1] // heads
    half = w_gate_hbm.shape[2]
    whole = half // WIDE * WIDE
    rest = half - whole
    columns = w_down_hbm.shape[2]
    cap_rows = zs * capacity
    tile = width // PROJ_TILES
    other_ctx = 1 - ctx

    def ahead(d):
        return lax.rem(level + d, zs)

    def behind(d):
        return lax.rem(level + zs - d, zs)

    def device(at_ctx, at_level, at_core):
        return {"ctx": at_ctx, "exp": at_level * 2 + at_core}

    core_partner = device(ctx, level, 1 - core)
    ctx_partner = device(other_ctx, level, core)

    loads = [
        pltpu.make_async_copy(out_proj_hbm, out_proj, load_sem.at[0]),
        pltpu.make_async_copy(w_gate_hbm.at[0, :, pl.ds(0, whole)], w_gate, load_sem.at[1]),
        pltpu.make_async_copy(w_up_hbm.at[0, :, pl.ds(0, whole)], w_up, load_sem.at[2]),
        pltpu.make_async_copy(
            w_gate_hbm.at[0, :, pl.ds(whole, rest)], w_rest.at[:, pl.ds(0, rest)], load_sem.at[3]
        ),
        pltpu.make_async_copy(
            w_up_hbm.at[0, :, pl.ds(whole, rest)], w_rest.at[:, pl.ds(rest, rest)], load_sem.at[4]
        ),
        pltpu.make_async_copy(w_down_hbm.at[0], w_down, load_sem.at[5]),
    ]
    for load in loads:
        load.start()

    barrier = pltpu.get_barrier_semaphore()
    peers = [core_partner, ctx_partner]
    for d in range(1, zs):
        peers.append(device(ctx, ahead(d), core))
        peers.append(device(other_ctx, ahead(d), core))
    for peer in peers:
        pl.semaphore_signal(barrier, inc=1, device_id=peer, device_id_type=MESH)

    def send(source, target, send_sem, recv_sem, peer):
        copy = pltpu.make_async_remote_copy(
            src_ref=source,
            dst_ref=target,
            send_sem=send_sem,
            recv_sem=recv_sem,
            device_id=peer,
            device_id_type=MESH,
        )
        copy.start()
        return copy

    sent = []
    lane = lax.broadcasted_iota(jnp.int32, (row_count, 128), 1)
    diagonal = lax.broadcasted_iota(jnp.int32, (row_count, row_count), 0) == lax.broadcasted_iota(
        jnp.int32, (row_count, row_count), 1
    )

    def upright_pair(flat):
        return [
            jnp.sum(jnp.where(diagonal, flat[k : k + 1, :], 0.0), axis=1, keepdims=True)
            for k in range(2)
        ]

    own_routes = upright_pair(routes[...].astype(jnp.float32))
    own_weight = upright_pair(route_weight[...])
    info[0, 0] = jnp.where(
        lane == 0,
        own_routes[0],
        jnp.where(lane == 1, own_routes[1], jnp.where(lane == 2, own_weight[0], own_weight[1])),
    )

    later_row = lax.broadcasted_iota(jnp.int32, (tokens, tokens), 0)
    later_col = lax.broadcasted_iota(jnp.int32, (tokens, tokens), 1)
    causal = later_row >= later_col
    sums = []
    for h in range(heads):
        span = pl.ds(h * head_width, head_width)
        spread = jnp.broadcast_to(log_decay[h : h + 1, :], (tokens, tokens))
        upright = jnp.transpose(spread)
        cum_col = jnp.sum(jnp.where(causal, spread, 0.0), axis=1, keepdims=True)
        cum_row = jnp.sum(jnp.where(later_row <= later_col, upright, 0.0), axis=0, keepdims=True)
        sums.append((cum_col, cum_row))
        tail = jnp.exp(cum_row[:, tokens - 1 : tokens] - cum_row)
        key_up = jnp.transpose(keys[:, span].astype(jnp.float32)) * tail
        state_out[h] = dot32(key_up.astype(jnp.bfloat16), values[:, span]).astype(jnp.bfloat16)

    pl.semaphore_wait(barrier, len(peers))
    state_copy = send(state_out, state_in, one_send.at[0], one_recv.at[0], ctx_partner)
    infos = []
    for rel in range(2):
        for d in range(zs):
            if rel or d:
                infos.append(
                    send(
                        info.at[0, 0],
                        info.at[rel, d],
                        info_send.at[rel * zs + d],
                        info_recv.at[rel * zs + d],
                        device(other_ctx if rel else ctx, ahead(d), core),
                    )
                )
    inner = []
    for h in range(heads):
        span = pl.ds(h * head_width, head_width)
        cum_col, cum_row = sums[h]
        scores = lax.dot_general(
            queries[:, span],
            keys[:, span],
            (((1,), (1,)), ((), ())),
            preferred_element_type=jnp.float32,
        )
        decay = jnp.where(causal, jnp.exp(jnp.minimum(cum_col - cum_row, 0.0)), 0.0)
        inner.append(dot32((scores * decay).astype(jnp.bfloat16), values[:, span]))
    state_copy.wait_recv()
    for h in range(heads):
        span = pl.ds(h * head_width, head_width)
        earlier = dot32(queries[:, span], state_in[h]) * jnp.exp(sums[h][0])
        attended = inner[h] + jnp.where(ctx == 0, 0.0, earlier)
        scale = lax.rsqrt(jnp.mean(attended * attended, axis=-1, keepdims=True) + 1e-06)
        opening = jax.nn.sigmoid(out_gate[:, span].astype(jnp.float32))
        gated[:, span] = (opening * attended * scale * attn_gain[:, span]).astype(jnp.bfloat16)

    order = [
        gated[pl.ds(pl.multiple_of(2 * row_count * ahead(d) + row_count * side, row_count), row_count), :]
        for side in (1 - core, core)
        for d in range(zs)
    ]
    ordered = jnp.concatenate(order, axis=0)
    loads[0].wait()
    split = zs * row_count
    pairs = []
    mine = []
    for n in range(PROJ_TILES):
        product = dot32(ordered, out_proj[:, n * tile : (n + 1) * tile])
        pair_out[n] = product[:split].astype(jnp.bfloat16)
        pairs.append(send(pair_out.at[n], pair_in.at[n], pair_send.at[n], pair_recv.at[n], core_partner))
        mine.append(product[split:])
    projected = []
    for n in range(PROJ_TILES):
        pairs[n].wait_recv()
        total = mine[n] + pair_in[n].astype(jnp.float32)
        for d in range(1, zs):
            proj_out[n, d] = total[d * row_count : (d + 1) * row_count].astype(jnp.bfloat16)
            projected.append(
                send(
                    proj_out.at[n, d],
                    proj_in.at[n, d],
                    proj_send.at[n * zs + d],
                    proj_recv.at[n * zs + d],
                    device(ctx, ahead(d), core),
                )
            )
        part = slice(n * tile, (n + 1) * tile)
        resid[:, part] = resid_in[:, part].astype(jnp.float32) + total[:row_count]

    for copy in infos:
        copy.wait_recv()
    block = row_count
    routed = info[...].reshape(2 * zs * block, 128)
    routed_up = jnp.transpose(routed)
    mark = level.astype(jnp.float32)
    count = 2 * zs * block
    place_row = lax.broadcasted_iota(jnp.int32, (count, count), 0)
    place_col = lax.broadcasted_iota(jnp.int32, (count, count), 1)
    same = place_row // block == place_col // block
    hit_col = jnp.where((routed[:, 0:1] == mark) | (routed[:, 1:2] == mark), 1.0, 0.0)
    hit_row = jnp.where((routed_up[0:1] == mark) | (routed_up[1:2] == mark), 1.0, 0.0)
    slot_row = jnp.sum(
        jnp.where(same & (place_row < place_col), hit_col, 0.0), axis=0, keepdims=True
    ).astype(jnp.int32)
    slot_col = jnp.sum(
        jnp.where(same & (place_col < place_row), hit_row, 0.0), axis=1, keepdims=True
    ).astype(jnp.int32)
    index_row = lax.broadcasted_iota(jnp.int32, (1, count), 1) // block * capacity + slot_row
    index_col = lax.broadcasted_iota(jnp.int32, (count, 1), 0) // block * capacity + slot_col
    reach_rows = lax.broadcasted_iota(jnp.int32, (cap_rows, count), 0)
    picker = jnp.where((reach_rows == index_row) & (hit_row > 0.5), 1.0, 0.0).astype(jnp.bfloat16)
    reach_cols = lax.broadcasted_iota(jnp.int32, (count, 2 * cap_rows), 1)
    placer = jnp.where((reach_cols == index_col) & (hit_col > 0.5), 1.0, 0.0).astype(jnp.bfloat16)

    for n in range(PROJ_TILES):
        part = slice(n * tile, (n + 1) * tile)
        for d in range(1, zs):
            projected[n * (zs - 1) + d - 1].wait_recv()
            resid[:, part] += proj_in[n, d].astype(jnp.float32)
    settled = resid[...].astype(jnp.bfloat16).astype(jnp.float32)
    resid[...] = settled
    scale = lax.rsqrt(jnp.mean(settled * settled, axis=-1, keepdims=True) + 1e-06)
    rows_in[0] = (settled * scale * moe_gain[...]).astype(jnp.bfloat16)

    def cut(n):
        return pl.ds(n * tile, tile)

    gathers = [
        [
            send(
                rows_in.at[0, :, cut(n)],
                rows_in.at[d, :, cut(n)],
                gather_send.at[n * zs + d],
                gather_recv.at[n * zs + d],
                device(ctx, ahead(d), core),
            )
            for d in range(1, zs)
        ]
        for n in range(PROJ_TILES)
    ]
    to_ctx, to_core, passed = [], [], []

    def pass_on(n):
        to_ctx[n].wait_recv()
        passed.append(
            send(
                picked.at[1, 0, :, cut(n)],
                picked.at[1, 1, :, cut(n)],
                pass_send.at[n],
                pass_recv.at[n],
                core_partner,
            )
        )

    for n in range(PROJ_TILES):
        for copy in gathers[n]:
            copy.wait_recv()
        landed = rows_in[:, :, n * tile : (n + 1) * tile].reshape(zs * block, tile)
        picked[0, 0, :, cut(n)] = dot32(picker[:, : zs * block], landed).astype(jnp.bfloat16)
        source = picked.at[0, 0, :, cut(n)]
        to_ctx.append(
            send(source, picked.at[1, 0, :, cut(n)], ctx_send.at[n], ctx_recv.at[n], ctx_partner)
        )
        to_core.append(
            send(source, picked.at[0, 1, :, cut(n)], core_send.at[n], core_recv.at[n], core_partner)
        )
    for n in range(PROJ_TILES - 1):
        pass_on(n)
    for copy in to_core:
        copy.wait_recv()

    def activate(gate_part, up_part):
        return (jax.nn.silu(gate_part) * up_part).astype(jnp.bfloat16)

    def hide(rel):
        def step(n, carry):
            span = pl.ds(pl.multiple_of(n * WIDE, WIDE), WIDE)
            rows = picked[rel].reshape(2 * cap_rows, width)
            hidden_own[rel, :, span] = activate(
                dot32(rows, w_gate[:, span]), dot32(rows, w_up[:, span])
            )
            return carry

        lax.fori_loop(0, whole // WIDE, step, 0)
        both = dot32(picked[rel].reshape(2 * cap_rows, width), w_rest[...])
        hidden_own[rel, :, whole:] = activate(both[:, :rest], both[:, rest:])
        return send(
            hidden_own.at[rel],
            hidden_in.at[1 - rel],
            hidden_send.at[rel],
            hidden_recv.at[1 - rel],
            ctx_partner,
        )

    def lower(rel, first):
        source = hidden_own if first else hidden_in
        side = ctx if first else other_ctx

        def step(n, carry):
            span = pl.ds(pl.multiple_of(n * WIDE, WIDE), WIDE)
            product = dot32(
                source[rel], w_down[pl.ds(pl.multiple_of(side * half, 128), half), span]
            )
            if first:
                expert_sum[rel, :, span] = product
            else:
                expert_sum[rel, :, span] += product
            return carry

        lax.fori_loop(0, columns // WIDE, step, 0)

    for load in loads[1:5]:
        load.wait()
    hidden_near = hide(0)
    pass_on(PROJ_TILES - 1)
    for copy in passed:
        copy.wait_recv()
    hidden_far = hide(1)
    loads[5].wait()
    lower(0, True)
    lower(1, True)

    def incoming_hidden(rel):
        return pltpu.make_async_remote_copy(
            src_ref=hidden_own.at[1 - rel],
            dst_ref=hidden_in.at[rel],
            send_sem=hidden_send.at[1 - rel],
            recv_sem=hidden_recv.at[rel],
            device_id=ctx_partner,
            device_id_type=MESH,
        )

    halves = [None, None]
    backs = {}
    for rel in (1, 0):
        incoming_hidden(rel).wait_recv()
        lower(rel, False)
        half_out[rel] = expert_sum[rel, cap_rows:, :].astype(jnp.bfloat16)
        halves[rel] = send(
            half_out.at[rel], half_in.at[rel], half_send.at[rel], half_recv.at[rel], core_partner
        )
        halves[rel].wait_recv()
        total = (expert_sum[rel, :cap_rows, :] + half_in[rel].astype(jnp.float32)).astype(jnp.bfloat16)
        chosen = placer[rel * zs * block : (rel + 1) * zs * block, rel * cap_rows : (rel + 1) * cap_rows]
        spread_rows = dot32(chosen, total).astype(jnp.bfloat16)
        back_in[rel, 0] = spread_rows[:block]
        for d in range(1, zs):
            back_out[rel, d] = spread_rows[d * block : (d + 1) * block]
            backs[rel, d] = send(
                back_out.at[rel, d],
                back_in.at[rel, d],
                back_send.at[rel * zs + d],
                back_recv.at[rel * zs + d],
                device(ctx, behind(d), core),
            )

    def mix(rel):
        table = info[rel, 0]
        total = jnp.zeros((block, columns), jnp.float32)
        for d in range(zs):
            if d:
                backs[rel, d].wait_recv()
            expert = ahead(d).astype(jnp.float32)
            weight = jnp.where(table[:, 0:1] == expert, table[:, 2:3], 0.0) + jnp.where(
                table[:, 1:2] == expert, table[:, 3:4], 0.0
            )
            total = total + weight * back_in[rel, d].astype(jnp.float32)
        return total

    last_out[...] = mix(1).astype(jnp.bfloat16)
    last = send(last_out, last_in, one_send.at[1], one_recv.at[1], ctx_partner)
    near = pl.ds(pl.multiple_of(ctx * columns, 128), columns)
    far = pl.ds(pl.multiple_of(other_ctx * columns, 128), columns)
    mixed[:, near] = (resid[:, near] + mix(0)).astype(jnp.bfloat16)
    last.wait_recv()
    mixed[:, far] = (resid[:, far] + last_in[...].astype(jnp.float32)).astype(jnp.bfloat16)

    sent += [state_copy, hidden_near, hidden_far, last] + to_ctx + to_core + passed
    sent += sum(gathers, [])
    for copy in sent + infos + pairs + projected + halves + list(backs.values()):
        copy.wait_send()


def per_device_kernel(
    resid_in,
    queries,
    keys,
    values,
    out_gate,
    log_decay,
    attn_gain,
    out_proj,
    moe_gain,
    routes,
    route_weight,
    w_gate,
    w_up,
    w_down,
):
    zs = lax.axis_size("exp") // 2
    row_count, width = resid_in.shape
    tokens = queries.shape[0]
    heads = log_decay.shape[0]
    head_width = queries.shape[1] // heads
    capacity = min(row_count, 6 * tokens // (4 * zs * zs))
    cap_rows = zs * capacity
    half = w_gate.shape[2]
    whole = half // WIDE * WIDE
    rest = half - whole
    columns = w_down.shape[2]
    tile = width // PROJ_TILES
    low = jnp.bfloat16
    dma = pltpu.SemaphoreType.DMA
    vmem = pl.BlockSpec(memory_space=pltpu.VMEM)
    away = pl.BlockSpec(memory_space=pl.ANY)
    return pl.pallas_call(
        functools.partial(layer_kernel, zs, capacity),
        out_shape=jax.ShapeDtypeStruct((row_count, width), low),
        in_specs=[vmem] * 7 + [away] + [vmem] * 3 + [away] * 3,
        out_specs=vmem,
        scratch_shapes=[
            pltpu.VMEM(out_proj.shape, low),
            pltpu.VMEM((width, whole), low),
            pltpu.VMEM((width, whole), low),
            pltpu.VMEM((width, 2 * rest), low),
            pltpu.VMEM(w_down.shape[1:], low),
            pltpu.VMEM((2, zs, row_count, 128), jnp.float32),
            pltpu.VMEM((heads, head_width, head_width), low),
            pltpu.VMEM((heads, head_width, head_width), low),
            pltpu.VMEM(queries.shape, low),
            pltpu.VMEM((PROJ_TILES, zs * row_count, tile), low),
            pltpu.VMEM((PROJ_TILES, zs * row_count, tile), low),
            pltpu.VMEM((PROJ_TILES, zs, row_count, tile), low),
            pltpu.VMEM((PROJ_TILES, zs, row_count, tile), low),
            pltpu.VMEM((row_count, width), jnp.float32),
            pltpu.VMEM((zs, row_count, width), low),
            pltpu.VMEM((2, 2, cap_rows, width), low),
            pltpu.VMEM((2, 2 * cap_rows, half), low),
            pltpu.VMEM((2, 2 * cap_rows, half), low),
            pltpu.VMEM((2, 2 * cap_rows, columns), jnp.float32),
            pltpu.VMEM((2, cap_rows, columns), low),
            pltpu.VMEM((2, cap_rows, columns), low),
            pltpu.VMEM((2, zs, row_count, columns), low),
            pltpu.VMEM((2, zs, row_count, columns), low),
            pltpu.VMEM((row_count, columns), low),
            pltpu.VMEM((row_count, columns), low),
            dma((6,)),
            dma((2 * zs,)),
            dma((2 * zs,)),
            dma((2,)),
            dma((2,)),
            dma((PROJ_TILES,)),
            dma((PROJ_TILES,)),
            dma((PROJ_TILES * zs,)),
            dma((PROJ_TILES * zs,)),
            dma((PROJ_TILES * zs,)),
            dma((PROJ_TILES * zs,)),
            dma((PROJ_TILES,)),
            dma((PROJ_TILES,)),
            dma((PROJ_TILES,)),
            dma((PROJ_TILES,)),
            dma((PROJ_TILES,)),
            dma((PROJ_TILES,)),
            dma((2,)),
            dma((2,)),
            dma((2,)),
            dma((2,)),
            dma((2 * zs,)),
            dma((2 * zs,)),
        ],
        compiler_params=pltpu.CompilerParams(
            collective_id=0, has_side_effects=True, vmem_limit_bytes=56 * 1024 * 1024
        ),
        cost_estimate=pl.CostEstimate(
            flops=12 * cap_rows * width * half * 2, bytes_accessed=6 * width * half, transcendentals=0
        ),
    )(
        resid_in,
        queries,
        keys,
        values,
        out_gate,
        log_decay,
        attn_gain.reshape(1, -1),
        out_proj,
        moe_gain.reshape(1, -1),
        routes.T,
        route_weight.T,
        w_gate,
        w_up,
        w_down,
    )


def solution(mesh):
    pairs_of_two = mesh.shape["ctx"] == 2 and mesh.shape["exp"] % 2 == 0
    return jax.shard_map(
        per_device_kernel if pairs_of_two else per_device,
        mesh=mesh,
        in_specs=(
            P(("groups", "ctx", "exp"), None),
            P(("groups", "ctx"), "exp"),
            P(("groups", "ctx"), "exp"),
            P(("groups", "ctx"), "exp"),
            P(("groups", "ctx"), "exp"),
            P("exp", ("groups", "ctx")),
            P("exp"),
            P("exp", None),
            P(),
            P(("groups", "ctx", "exp"), None),
            P(("groups", "ctx", "exp"), None),
            P("exp", None, "ctx"),
            P("exp", None, "ctx"),
            P("exp", None, "ctx"),
        ),
        out_specs=P(("groups", "ctx", "exp"), None),
        check_vma=False,
    )
```

```python
import functools

import jax
import jax.numpy as jnp
from jax import lax
from jax.experimental import pallas as pl
from jax.experimental.pallas import tpu as pltpu
from jax.sharding import PartitionSpec as P

HIGHEST = lax.Precision.HIGHEST


def from_behind(block, axis, distance):
    devices = range(lax.axis_size(axis))
    route = [(i - distance, i) for i in devices if i - distance in devices]
    return lax.ppermute(block, axis, route)


def local_terms(query_block, key_block, value_block, log_rates):
    cumulative = jnp.cumsum(log_rates, axis=1)
    scores = jnp.einsum("thd,shd->hts", query_block, key_block, preferred_element_type=jnp.float32)
    length = log_rates.shape[1]
    later = (
        jnp.arange(length, dtype=jnp.int32)[:, None] >= jnp.arange(length, dtype=jnp.int32)[None, :]
    )
    spread = cumulative[:, :, None] - cumulative[:, None, :]
    weights = jnp.where(later[None], jnp.exp(jnp.minimum(spread, 0.0)), 0.0)
    value_float = value_block.astype(jnp.float32)
    inner_part = jnp.einsum("hts,shd->thd", scores * weights, value_float, precision=HIGHEST)
    tail_decay = jnp.exp(cumulative[:, -1:] - cumulative)
    key_scaled = key_block.astype(jnp.float32) * jnp.transpose(tail_decay)[:, :, None]
    local_state = jnp.einsum("shd,she->hde", key_scaled, value_float, precision=HIGHEST)
    query_scaled = query_block.astype(jnp.float32) * jnp.transpose(jnp.exp(cumulative))[:, :, None]
    return (inner_part, query_scaled, local_state, jnp.exp(cumulative[:, -1]))


def head_gate(attended, out_gate, attn_gain):
    token_count, head_count, head_width = attended.shape
    scale_rows = lax.rsqrt(jnp.mean(attended * attended, axis=-1, keepdims=True) + 1e-06)
    gain_table = attn_gain.reshape(head_count, head_width)
    opening = jax.nn.sigmoid(out_gate.astype(jnp.float32)).reshape(attended.shape)
    gated = opening * attended * scale_rows * gain_table
    return gated.reshape(token_count, head_count * head_width).astype(jnp.bfloat16)


def rms_rows(rows_in, gain):
    values_float = rows_in.astype(jnp.float32)
    scale_rows = lax.rsqrt(jnp.mean(values_float * values_float, axis=-1, keepdims=True) + 1e-06)
    return (values_float * scale_rows * gain).astype(jnp.bfloat16)


def slot_tables(route_rows, expert_count, capacity):
    leading = route_rows.shape[:-2]
    pair_ids = route_rows.reshape(leading + (-1,))
    onehot = (pair_ids[..., None] == jnp.arange(expert_count, dtype=jnp.int32)).astype(jnp.int32)
    earlier = jnp.cumsum(onehot, axis=-2) - onehot
    slot_ids = jnp.sum(earlier * onehot, axis=-1)
    slot_hit = (slot_ids[..., None] == jnp.arange(capacity, dtype=jnp.int32)).astype(jnp.float32)
    expert_hit = onehot.astype(jnp.float32).reshape(route_rows.shape + (expert_count,))
    return (expert_hit, slot_hit.reshape(route_rows.shape + (capacity,)))


def per_device(
    resid_in,
    queries,
    keys,
    values,
    out_gate,
    log_decay,
    attn_gain,
    out_proj,
    moe_gain,
    routes,
    route_weight,
    w_gate,
    w_up,
    w_down,
):
    head_count = log_decay.shape[0]
    token_count = queries.shape[0]
    head_width = queries.shape[1] // head_count
    shaped = (token_count, head_count, head_width)
    inner_part, query_scaled, local_state, block_decay = local_terms(
        queries.reshape(shaped), keys.reshape(shaped), values.reshape(shaped), log_decay
    )
    ctx_size = lax.axis_size("ctx")
    exp_size = lax.axis_size("exp")
    empty_state = jnp.zeros_like(local_state)

    def advance(turn_index, incoming):
        carried = block_decay[:, None, None] * incoming + local_state
        return from_behind(carried, "ctx", 1)

    incoming = lax.fori_loop(0, ctx_size - 1, advance, empty_state)
    attended = inner_part + jnp.einsum("thd,hde->the", query_scaled, incoming, precision=HIGHEST)
    gated = head_gate(attended, out_gate, attn_gain)
    attn_sum = lax.psum_scatter(
        jnp.dot(gated, out_proj, preferred_element_type=jnp.float32),
        "exp",
        scatter_dimension=0,
        tiled=True,
    )
    resid = (resid_in.astype(jnp.float32) + attn_sum).astype(jnp.bfloat16)
    normed = rms_rows(resid, moe_gain)
    row_count = resid.shape[0]
    expert_count = exp_size // 2
    capacity = min(row_count, 6 * token_count // (exp_size * exp_size))
    hit_expert, hit_slot = slot_tables(routes, expert_count, capacity)
    gate_local = w_gate[0]
    up_local = w_up[0]
    down_local = w_down[0]
    all_rows, all_routes = (
        lax.all_gather(normed[None], "ctx", axis=0, tiled=True),
        lax.all_gather(routes[None], "ctx", axis=0, tiled=True),
    )
    every_expert, every_slot = slot_tables(all_routes, expert_count, capacity)
    picker = jnp.repeat(jnp.einsum("crke,crks->cesr", every_expert, every_slot), 2, axis=1).astype(
        jnp.bfloat16
    )
    outgoing = jnp.einsum(
        "cosr,crd->cosd", picker, all_rows, preferred_element_type=jnp.float32
    ).astype(jnp.bfloat16)
    arrived = lax.all_to_all(outgoing, "exp", split_axis=1, concat_axis=1, tiled=True)
    gate_part = jnp.einsum("abcd,dh->abch", arrived, gate_local, preferred_element_type=jnp.float32)
    up_part = jnp.einsum("abcd,dh->abch", arrived, up_local, preferred_element_type=jnp.float32)
    hidden = (jax.nn.silu(gate_part) * up_part).astype(jnp.bfloat16)
    partial_out = jnp.einsum(
        "abch,hn->abcn",
        lax.all_gather(hidden, "ctx", axis=3, tiled=True),
        down_local,
        preferred_element_type=jnp.float32,
    )
    came_back = lax.all_to_all(
        lax.all_to_all(partial_out, "ctx", split_axis=0, concat_axis=3, tiled=True),
        "exp",
        split_axis=1,
        concat_axis=1,
        tiled=True,
    )
    halves = came_back[0].reshape(expert_count, 2, capacity, came_back.shape[-1])
    paired = halves[:, 0] + halves[:, 1]
    mixing = jnp.einsum("rk,rke,rks->res", route_weight, hit_expert, hit_slot)
    moe_sum = jnp.einsum("res,esd->rd", mixing, paired, precision=HIGHEST)
    return (resid.astype(jnp.float32) + moe_sum).astype(jnp.bfloat16)


MESH = pl.DeviceIdType.MESH
PROJ_TILES = 3
WIDE = 256


def dot32(left, right):
    return jnp.dot(left, right, preferred_element_type=jnp.float32)


def layer_kernel(
    zs,
    capacity,
    resid_in,
    queries,
    keys,
    values,
    out_gate,
    log_decay,
    attn_gain,
    out_proj_hbm,
    moe_gain,
    routes,
    route_weight,
    w_gate_hbm,
    w_up_hbm,
    w_down_hbm,
    mixed,
    out_proj,
    w_gate,
    w_up,
    w_rest,
    w_down,
    info,
    state_out,
    state_in,
    gated,
    pair_out,
    pair_in,
    proj_out,
    proj_in,
    resid,
    rows_in,
    picked,
    hidden_own,
    hidden_in,
    expert_sum,
    half_out,
    half_in,
    back_out,
    back_in,
    last_out,
    last_in,
    load_sem,
    info_send,
    info_recv,
    one_send,
    one_recv,
    pair_send,
    pair_recv,
    proj_send,
    proj_recv,
    gather_send,
    gather_recv,
    ctx_send,
    ctx_recv,
    core_send,
    core_recv,
    pass_send,
    pass_recv,
    hidden_send,
    hidden_recv,
    half_send,
    half_recv,
    back_send,
    back_recv,
):
    ctx = lax.axis_index("ctx")
    exp = lax.axis_index("exp")
    core = lax.rem(exp, 2)
    level = exp // 2
    row_count, width = resid_in.shape
    tokens = queries.shape[0]
    heads = log_decay.shape[0]
    head_width = queries.shape[1] // heads
    half = w_gate_hbm.shape[2]
    whole = half // WIDE * WIDE
    rest = half - whole
    columns = w_down_hbm.shape[2]
    cap_rows = zs * capacity
    tile = width // PROJ_TILES
    other_ctx = 1 - ctx

    def ahead(d):
        return lax.rem(level + d, zs)

    def behind(d):
        return lax.rem(level + zs - d, zs)

    def device(at_ctx, at_level, at_core):
        return {"ctx": at_ctx, "exp": at_level * 2 + at_core}

    core_partner = device(ctx, level, 1 - core)
    ctx_partner = device(other_ctx, level, core)

    loads = [
        pltpu.make_async_copy(out_proj_hbm, out_proj, load_sem.at[0]),
        pltpu.make_async_copy(w_gate_hbm.at[0, :, pl.ds(0, whole)], w_gate, load_sem.at[1]),
        pltpu.make_async_copy(w_up_hbm.at[0, :, pl.ds(0, whole)], w_up, load_sem.at[2]),
        pltpu.make_async_copy(
            w_gate_hbm.at[0, :, pl.ds(whole, rest)], w_rest.at[:, pl.ds(0, rest)], load_sem.at[3]
        ),
        pltpu.make_async_copy(
            w_up_hbm.at[0, :, pl.ds(whole, rest)], w_rest.at[:, pl.ds(rest, rest)], load_sem.at[4]
        ),
        pltpu.make_async_copy(w_down_hbm.at[0], w_down, load_sem.at[5]),
    ]
    for load in loads:
        load.start()

    barrier = pltpu.get_barrier_semaphore()
    peers = [core_partner, ctx_partner]
    for d in range(1, zs):
        peers.append(device(ctx, ahead(d), core))
        peers.append(device(other_ctx, ahead(d), core))
    for peer in peers:
        pl.semaphore_signal(barrier, inc=1, device_id=peer, device_id_type=MESH)

    def send(source, target, send_sem, recv_sem, peer):
        copy = pltpu.make_async_remote_copy(
            src_ref=source,
            dst_ref=target,
            send_sem=send_sem,
            recv_sem=recv_sem,
            device_id=peer,
            device_id_type=MESH,
        )
        copy.start()
        return copy

    sent = []
    lane = lax.broadcasted_iota(jnp.int32, (row_count, 128), 1)
    diagonal = lax.broadcasted_iota(jnp.int32, (row_count, row_count), 0) == lax.broadcasted_iota(
        jnp.int32, (row_count, row_count), 1
    )

    def upright_pair(flat):
        return [
            jnp.sum(jnp.where(diagonal, flat[k : k + 1, :], 0.0), axis=1, keepdims=True)
            for k in range(2)
        ]

    own_routes = upright_pair(routes[...].astype(jnp.float32))
    own_weight = upright_pair(route_weight[...])
    info[0, 0] = jnp.where(
        lane == 0,
        own_routes[0],
        jnp.where(lane == 1, own_routes[1], jnp.where(lane == 2, own_weight[0], own_weight[1])),
    )

    later_row = lax.broadcasted_iota(jnp.int32, (tokens, tokens), 0)
    later_col = lax.broadcasted_iota(jnp.int32, (tokens, tokens), 1)
    causal = later_row >= later_col
    sums = []
    for h in range(heads):
        span = pl.ds(h * head_width, head_width)
        spread = jnp.broadcast_to(log_decay[h : h + 1, :], (tokens, tokens))
        upright = jnp.transpose(spread)
        cum_col = jnp.sum(jnp.where(causal, spread, 0.0), axis=1, keepdims=True)
        cum_row = jnp.sum(jnp.where(later_row <= later_col, upright, 0.0), axis=0, keepdims=True)
        sums.append((cum_col, cum_row))
        tail = jnp.exp(cum_row[:, tokens - 1 : tokens] - cum_row)
        key_up = jnp.transpose(keys[:, span].astype(jnp.float32)) * tail
        state_out[h] = dot32(key_up.astype(jnp.bfloat16), values[:, span]).astype(jnp.bfloat16)

    pl.semaphore_wait(barrier, len(peers))
    state_copy = send(state_out, state_in, one_send.at[0], one_recv.at[0], ctx_partner)
    infos = []
    for rel in range(2):
        for d in range(zs):
            if rel or d:
                infos.append(
                    send(
                        info.at[0, 0],
                        info.at[rel, d],
                        info_send.at[rel * zs + d],
                        info_recv.at[rel * zs + d],
                        device(other_ctx if rel else ctx, ahead(d), core),
                    )
                )
    inner = []
    for h in range(heads):
        span = pl.ds(h * head_width, head_width)
        cum_col, cum_row = sums[h]
        scores = lax.dot_general(
            queries[:, span],
            keys[:, span],
            (((1,), (1,)), ((), ())),
            preferred_element_type=jnp.float32,
        )
        decay = jnp.where(causal, jnp.exp(jnp.minimum(cum_col - cum_row, 0.0)), 0.0)
        inner.append(dot32((scores * decay).astype(jnp.bfloat16), values[:, span]))
    state_copy.wait_recv()
    for h in range(heads):
        span = pl.ds(h * head_width, head_width)
        earlier = dot32(queries[:, span], state_in[h]) * jnp.exp(sums[h][0])
        attended = inner[h] + jnp.where(ctx == 0, 0.0, earlier)
        scale = lax.rsqrt(jnp.mean(attended * attended, axis=-1, keepdims=True) + 1e-06)
        opening = jax.nn.sigmoid(out_gate[:, span].astype(jnp.float32))
        gated[:, span] = (opening * attended * scale * attn_gain[:, span]).astype(jnp.bfloat16)

    order = [
        gated[pl.ds(pl.multiple_of(2 * row_count * ahead(d) + row_count * side, row_count), row_count), :]
        for side in (1 - core, core)
        for d in range(zs)
    ]
    ordered = jnp.concatenate(order, axis=0)
    loads[0].wait()
    split = zs * row_count
    pairs = []
    mine = []
    for n in range(PROJ_TILES):
        product = dot32(ordered, out_proj[:, n * tile : (n + 1) * tile])
        pair_out[n] = product[:split].astype(jnp.bfloat16)
        pairs.append(send(pair_out.at[n], pair_in.at[n], pair_send.at[n], pair_recv.at[n], core_partner))
        mine.append(product[split:])
    projected = []
    for n in range(PROJ_TILES):
        pairs[n].wait_recv()
        total = mine[n] + pair_in[n].astype(jnp.float32)
        for d in range(1, zs):
            proj_out[n, d] = total[d * row_count : (d + 1) * row_count].astype(jnp.bfloat16)
            projected.append(
                send(
                    proj_out.at[n, d],
                    proj_in.at[n, d],
                    proj_send.at[n * zs + d],
                    proj_recv.at[n * zs + d],
                    device(ctx, ahead(d), core),
                )
            )
        part = slice(n * tile, (n + 1) * tile)
        resid[:, part] = resid_in[:, part].astype(jnp.float32) + total[:row_count]

    for copy in infos:
        copy.wait_recv()
    block = row_count
    routed = info[...].reshape(2 * zs * block, 128)
    routed_up = jnp.transpose(routed)
    mark = level.astype(jnp.float32)
    count = 2 * zs * block
    place_row = lax.broadcasted_iota(jnp.int32, (count, count), 0)
    place_col = lax.broadcasted_iota(jnp.int32, (count, count), 1)
    same = place_row // block == place_col // block
    hit_col = jnp.where((routed[:, 0:1] == mark) | (routed[:, 1:2] == mark), 1.0, 0.0)
    hit_row = jnp.where((routed_up[0:1] == mark) | (routed_up[1:2] == mark), 1.0, 0.0)
    slot_row = jnp.sum(
        jnp.where(same & (place_row < place_col), hit_col, 0.0), axis=0, keepdims=True
    ).astype(jnp.int32)
    slot_col = jnp.sum(
        jnp.where(same & (place_col < place_row), hit_row, 0.0), axis=1, keepdims=True
    ).astype(jnp.int32)
    index_row = lax.broadcasted_iota(jnp.int32, (1, count), 1) // block * capacity + slot_row
    index_col = lax.broadcasted_iota(jnp.int32, (count, 1), 0) // block * capacity + slot_col
    reach_rows = lax.broadcasted_iota(jnp.int32, (cap_rows, count), 0)
    picker = jnp.where((reach_rows == index_row) & (hit_row > 0.5), 1.0, 0.0).astype(jnp.bfloat16)
    reach_cols = lax.broadcasted_iota(jnp.int32, (count, 2 * cap_rows), 1)
    placer = jnp.where((reach_cols == index_col) & (hit_col > 0.5), 1.0, 0.0).astype(jnp.bfloat16)

    for n in range(PROJ_TILES):
        part = slice(n * tile, (n + 1) * tile)
        for d in range(1, zs):
            projected[n * (zs - 1) + d - 1].wait_recv()
            resid[:, part] += proj_in[n, d].astype(jnp.float32)
    settled = resid[...].astype(jnp.bfloat16).astype(jnp.float32)
    resid[...] = settled
    scale = lax.rsqrt(jnp.mean(settled * settled, axis=-1, keepdims=True) + 1e-06)
    rows_in[0] = (settled * scale * moe_gain[...]).astype(jnp.bfloat16)

    def cut(n):
        return pl.ds(n * tile, tile)

    gathers = [
        [
            send(
                rows_in.at[0, :, cut(n)],
                rows_in.at[d, :, cut(n)],
                gather_send.at[n * zs + d],
                gather_recv.at[n * zs + d],
                device(ctx, ahead(d), core),
            )
            for d in range(1, zs)
        ]
        for n in range(PROJ_TILES)
    ]
    to_ctx, to_core, passed = [], [], []

    def pass_on(n):
        to_ctx[n].wait_recv()
        passed.append(
            send(
                picked.at[1, 0, :, cut(n)],
                picked.at[1, 1, :, cut(n)],
                pass_send.at[n],
                pass_recv.at[n],
                core_partner,
            )
        )

    for n in range(PROJ_TILES):
        for copy in gathers[n]:
            copy.wait_recv()
        landed = rows_in[:, :, n * tile : (n + 1) * tile].reshape(zs * block, tile)
        picked[0, 0, :, cut(n)] = dot32(picker[:, : zs * block], landed).astype(jnp.bfloat16)
        source = picked.at[0, 0, :, cut(n)]
        to_ctx.append(
            send(source, picked.at[1, 0, :, cut(n)], ctx_send.at[n], ctx_recv.at[n], ctx_partner)
        )
        to_core.append(
            send(source, picked.at[0, 1, :, cut(n)], core_send.at[n], core_recv.at[n], core_partner)
        )
    for n in range(PROJ_TILES - 1):
        pass_on(n)
    for copy in to_core:
        copy.wait_recv()

    def activate(gate_part, up_part):
        return (jax.nn.silu(gate_part) * up_part).astype(jnp.bfloat16)

    early = whole // WIDE // 2
    hidden_cuts = [(0, early * WIDE), (early * WIDE, half - early * WIDE)]

    def exchange_hidden(rel, part):
        span = pl.ds(*hidden_cuts[part])
        return pltpu.make_async_remote_copy(
            src_ref=hidden_own.at[rel, :, span],
            dst_ref=hidden_in.at[1 - rel, :, span],
            send_sem=hidden_send.at[2 * rel + part],
            recv_sem=hidden_recv.at[2 * (1 - rel) + part],
            device_id=ctx_partner,
            device_id_type=MESH,
        )

    def hide(rel):
        def step(n, carry):
            span = pl.ds(pl.multiple_of(n * WIDE, WIDE), WIDE)
            rows = picked[rel].reshape(2 * cap_rows, width)
            hidden_own[rel, :, span] = activate(
                dot32(rows, w_gate[:, span]), dot32(rows, w_up[:, span])
            )
            return carry

        lax.fori_loop(0, early, step, 0)
        copies = [exchange_hidden(rel, 0)]
        copies[0].start()
        lax.fori_loop(early, whole // WIDE, step, 0)
        both = dot32(picked[rel].reshape(2 * cap_rows, width), w_rest[...])
        hidden_own[rel, :, whole:] = activate(both[:, :rest], both[:, rest:])
        copies.append(exchange_hidden(rel, 1))
        copies[1].start()
        return copies

    def lower(rel, first, start, size, tiles):
        source = hidden_own if first else hidden_in
        side = ctx if first else other_ctx

        def step(n, carry):
            span = pl.ds(pl.multiple_of(n * WIDE, WIDE), WIDE)
            product = dot32(
                source[rel, :, start : start + size],
                w_down[pl.ds(pl.multiple_of(side * half + start, 128), size), span],
            )
            if first:
                expert_sum[rel, :, span] = product
            else:
                expert_sum[rel, :, span] += product
            return carry

        lax.fori_loop(tiles[0], tiles[1], step, 0)

    for load in loads[1:5]:
        load.wait()
    hidden_near = hide(0)
    pass_on(PROJ_TILES - 1)
    for copy in passed:
        copy.wait_recv()
    hidden_far = hide(1)
    loads[5].wait()
    all_tiles = (0, columns // WIDE)
    middle = columns // WIDE // 2
    lower(0, True, 0, half, all_tiles)
    lower(1, True, 0, half, all_tiles)
    tile_cuts = [(0, middle), (middle, columns // WIDE)]

    halves = []
    backs = {}
    for rel in (1, 0):
        exchange_hidden(1 - rel, 0).wait_recv()
        lower(rel, False, *hidden_cuts[0], all_tiles)
        exchange_hidden(1 - rel, 1).wait_recv()
        for part in range(2):
            lower(rel, False, *hidden_cuts[1], tile_cuts[part])
            span = slice(tile_cuts[part][0] * WIDE, tile_cuts[part][1] * WIDE)
            half_out[rel, :, span] = expert_sum[rel, cap_rows:, span].astype(jnp.bfloat16)
            halves.append(
                send(
                    half_out.at[rel, :, span],
                    half_in.at[rel, :, span],
                    half_send.at[2 * rel + part],
                    half_recv.at[2 * rel + part],
                    core_partner,
                )
            )
        chosen = placer[rel * zs * block : (rel + 1) * zs * block, rel * cap_rows : (rel + 1) * cap_rows]
        for part in range(2):
            span = slice(tile_cuts[part][0] * WIDE, tile_cuts[part][1] * WIDE)
            halves[part - 2].wait_recv()
            total = expert_sum[rel, :cap_rows, span] + half_in[rel, :, span].astype(jnp.float32)
            spread_rows = dot32(chosen, total.astype(jnp.bfloat16)).astype(jnp.bfloat16)
            back_in[rel, 0, :, span] = spread_rows[:block]
            for d in range(1, zs):
                back_out[rel, d, :, span] = spread_rows[d * block : (d + 1) * block]
                backs[rel, d, part] = send(
                    back_out.at[rel, d, :, span],
                    back_in.at[rel, d, :, span],
                    back_send.at[(2 * rel + part) * zs + d],
                    back_recv.at[(2 * rel + part) * zs + d],
                    device(ctx, behind(d), core),
                )

    def mix(rel):
        table = info[rel, 0]
        total = jnp.zeros((block, columns), jnp.float32)
        for d in range(zs):
            if d:
                backs[rel, d, 0].wait_recv()
                backs[rel, d, 1].wait_recv()
            expert = ahead(d).astype(jnp.float32)
            weight = jnp.where(table[:, 0:1] == expert, table[:, 2:3], 0.0) + jnp.where(
                table[:, 1:2] == expert, table[:, 3:4], 0.0
            )
            total = total + weight * back_in[rel, d].astype(jnp.float32)
        return total

    last_out[...] = mix(1).astype(jnp.bfloat16)
    last = send(last_out, last_in, one_send.at[1], one_recv.at[1], ctx_partner)
    near = pl.ds(pl.multiple_of(ctx * columns, 128), columns)
    far = pl.ds(pl.multiple_of(other_ctx * columns, 128), columns)
    mixed[:, near] = (resid[:, near] + mix(0)).astype(jnp.bfloat16)
    last.wait_recv()
    mixed[:, far] = (resid[:, far] + last_in[...].astype(jnp.float32)).astype(jnp.bfloat16)

    sent += [state_copy, last] + hidden_near + hidden_far + to_ctx + to_core + passed
    sent += sum(gathers, [])
    for copy in sent + infos + pairs + projected + halves + list(backs.values()):
        copy.wait_send()


def per_device_kernel(
    resid_in,
    queries,
    keys,
    values,
    out_gate,
    log_decay,
    attn_gain,
    out_proj,
    moe_gain,
    routes,
    route_weight,
    w_gate,
    w_up,
    w_down,
):
    zs = lax.axis_size("exp") // 2
    row_count, width = resid_in.shape
    tokens = queries.shape[0]
    heads = log_decay.shape[0]
    head_width = queries.shape[1] // heads
    capacity = min(row_count, 6 * tokens // (4 * zs * zs))
    cap_rows = zs * capacity
    half = w_gate.shape[2]
    whole = half // WIDE * WIDE
    rest = half - whole
    columns = w_down.shape[2]
    tile = width // PROJ_TILES
    low = jnp.bfloat16
    dma = pltpu.SemaphoreType.DMA
    vmem = pl.BlockSpec(memory_space=pltpu.VMEM)
    away = pl.BlockSpec(memory_space=pl.ANY)
    return pl.pallas_call(
        functools.partial(layer_kernel, zs, capacity),
        out_shape=jax.ShapeDtypeStruct((row_count, width), low),
        in_specs=[vmem] * 7 + [away] + [vmem] * 3 + [away] * 3,
        out_specs=vmem,
        scratch_shapes=[
            pltpu.VMEM(out_proj.shape, low),
            pltpu.VMEM((width, whole), low),
            pltpu.VMEM((width, whole), low),
            pltpu.VMEM((width, 2 * rest), low),
            pltpu.VMEM(w_down.shape[1:], low),
            pltpu.VMEM((2, zs, row_count, 128), jnp.float32),
            pltpu.VMEM((heads, head_width, head_width), low),
            pltpu.VMEM((heads, head_width, head_width), low),
            pltpu.VMEM(queries.shape, low),
            pltpu.VMEM((PROJ_TILES, zs * row_count, tile), low),
            pltpu.VMEM((PROJ_TILES, zs * row_count, tile), low),
            pltpu.VMEM((PROJ_TILES, zs, row_count, tile), low),
            pltpu.VMEM((PROJ_TILES, zs, row_count, tile), low),
            pltpu.VMEM((row_count, width), jnp.float32),
            pltpu.VMEM((zs, row_count, width), low),
            pltpu.VMEM((2, 2, cap_rows, width), low),
            pltpu.VMEM((2, 2 * cap_rows, half), low),
            pltpu.VMEM((2, 2 * cap_rows, half), low),
            pltpu.VMEM((2, 2 * cap_rows, columns), jnp.float32),
            pltpu.VMEM((2, cap_rows, columns), low),
            pltpu.VMEM((2, cap_rows, columns), low),
            pltpu.VMEM((2, zs, row_count, columns), low),
            pltpu.VMEM((2, zs, row_count, columns), low),
            pltpu.VMEM((row_count, columns), low),
            pltpu.VMEM((row_count, columns), low),
            dma((6,)),
            dma((2 * zs,)),
            dma((2 * zs,)),
            dma((2,)),
            dma((2,)),
            dma((PROJ_TILES,)),
            dma((PROJ_TILES,)),
            dma((PROJ_TILES * zs,)),
            dma((PROJ_TILES * zs,)),
            dma((PROJ_TILES * zs,)),
            dma((PROJ_TILES * zs,)),
            dma((PROJ_TILES,)),
            dma((PROJ_TILES,)),
            dma((PROJ_TILES,)),
            dma((PROJ_TILES,)),
            dma((PROJ_TILES,)),
            dma((PROJ_TILES,)),
            dma((4,)),
            dma((4,)),
            dma((4,)),
            dma((4,)),
            dma((4 * zs,)),
            dma((4 * zs,)),
        ],
        compiler_params=pltpu.CompilerParams(
            collective_id=0, has_side_effects=True, vmem_limit_bytes=56 * 1024 * 1024
        ),
        cost_estimate=pl.CostEstimate(
            flops=12 * cap_rows * width * half * 2, bytes_accessed=6 * width * half, transcendentals=0
        ),
    )(
        resid_in,
        queries,
        keys,
        values,
        out_gate,
        log_decay,
        attn_gain.reshape(1, -1),
        out_proj,
        moe_gain.reshape(1, -1),
        routes.T,
        route_weight.T,
        w_gate,
        w_up,
        w_down,
    )


def solution(mesh):
    pairs_of_two = mesh.shape["ctx"] == 2 and mesh.shape["exp"] % 2 == 0
    return jax.shard_map(
        per_device_kernel if pairs_of_two else per_device,
        mesh=mesh,
        in_specs=(
            P(("groups", "ctx", "exp"), None),
            P(("groups", "ctx"), "exp"),
            P(("groups", "ctx"), "exp"),
            P(("groups", "ctx"), "exp"),
            P(("groups", "ctx"), "exp"),
            P("exp", ("groups", "ctx")),
            P("exp"),
            P("exp", None),
            P(),
            P(("groups", "ctx", "exp"), None),
            P(("groups", "ctx", "exp"), None),
            P("exp", None, "ctx"),
            P("exp", None, "ctx"),
            P("exp", None, "ctx"),
        ),
        out_specs=P(("groups", "ctx", "exp"), None),
        check_vma=False,
    )
```

```python
import functools

import jax
import jax.numpy as jnp
from jax import lax
from jax.experimental import pallas as pl
from jax.experimental.pallas import tpu as pltpu
from jax.sharding import PartitionSpec as P

HIGHEST = lax.Precision.HIGHEST


def from_behind(block, axis, distance):
    devices = range(lax.axis_size(axis))
    route = [(i - distance, i) for i in devices if i - distance in devices]
    return lax.ppermute(block, axis, route)


def local_terms(query_block, key_block, value_block, log_rates):
    cumulative = jnp.cumsum(log_rates, axis=1)
    scores = jnp.einsum("thd,shd->hts", query_block, key_block, preferred_element_type=jnp.float32)
    length = log_rates.shape[1]
    later = (
        jnp.arange(length, dtype=jnp.int32)[:, None] >= jnp.arange(length, dtype=jnp.int32)[None, :]
    )
    spread = cumulative[:, :, None] - cumulative[:, None, :]
    weights = jnp.where(later[None], jnp.exp(jnp.minimum(spread, 0.0)), 0.0)
    value_float = value_block.astype(jnp.float32)
    inner_part = jnp.einsum("hts,shd->thd", scores * weights, value_float, precision=HIGHEST)
    tail_decay = jnp.exp(cumulative[:, -1:] - cumulative)
    key_scaled = key_block.astype(jnp.float32) * jnp.transpose(tail_decay)[:, :, None]
    local_state = jnp.einsum("shd,she->hde", key_scaled, value_float, precision=HIGHEST)
    query_scaled = query_block.astype(jnp.float32) * jnp.transpose(jnp.exp(cumulative))[:, :, None]
    return (inner_part, query_scaled, local_state, jnp.exp(cumulative[:, -1]))


def head_gate(attended, out_gate, attn_gain):
    token_count, head_count, head_width = attended.shape
    scale_rows = lax.rsqrt(jnp.mean(attended * attended, axis=-1, keepdims=True) + 1e-06)
    gain_table = attn_gain.reshape(head_count, head_width)
    opening = jax.nn.sigmoid(out_gate.astype(jnp.float32)).reshape(attended.shape)
    gated = opening * attended * scale_rows * gain_table
    return gated.reshape(token_count, head_count * head_width).astype(jnp.bfloat16)


def rms_rows(rows_in, gain):
    values_float = rows_in.astype(jnp.float32)
    scale_rows = lax.rsqrt(jnp.mean(values_float * values_float, axis=-1, keepdims=True) + 1e-06)
    return (values_float * scale_rows * gain).astype(jnp.bfloat16)


def slot_tables(route_rows, expert_count, capacity):
    leading = route_rows.shape[:-2]
    pair_ids = route_rows.reshape(leading + (-1,))
    onehot = (pair_ids[..., None] == jnp.arange(expert_count, dtype=jnp.int32)).astype(jnp.int32)
    earlier = jnp.cumsum(onehot, axis=-2) - onehot
    slot_ids = jnp.sum(earlier * onehot, axis=-1)
    slot_hit = (slot_ids[..., None] == jnp.arange(capacity, dtype=jnp.int32)).astype(jnp.float32)
    expert_hit = onehot.astype(jnp.float32).reshape(route_rows.shape + (expert_count,))
    return (expert_hit, slot_hit.reshape(route_rows.shape + (capacity,)))


def per_device(
    resid_in,
    queries,
    keys,
    values,
    out_gate,
    log_decay,
    attn_gain,
    out_proj,
    moe_gain,
    routes,
    route_weight,
    w_gate,
    w_up,
    w_down,
):
    head_count = log_decay.shape[0]
    token_count = queries.shape[0]
    head_width = queries.shape[1] // head_count
    shaped = (token_count, head_count, head_width)
    inner_part, query_scaled, local_state, block_decay = local_terms(
        queries.reshape(shaped), keys.reshape(shaped), values.reshape(shaped), log_decay
    )
    ctx_size = lax.axis_size("ctx")
    exp_size = lax.axis_size("exp")
    empty_state = jnp.zeros_like(local_state)

    def advance(turn_index, incoming):
        carried = block_decay[:, None, None] * incoming + local_state
        return from_behind(carried, "ctx", 1)

    incoming = lax.fori_loop(0, ctx_size - 1, advance, empty_state)
    attended = inner_part + jnp.einsum("thd,hde->the", query_scaled, incoming, precision=HIGHEST)
    gated = head_gate(attended, out_gate, attn_gain)
    attn_sum = lax.psum_scatter(
        jnp.dot(gated, out_proj, preferred_element_type=jnp.float32),
        "exp",
        scatter_dimension=0,
        tiled=True,
    )
    resid = (resid_in.astype(jnp.float32) + attn_sum).astype(jnp.bfloat16)
    normed = rms_rows(resid, moe_gain)
    row_count = resid.shape[0]
    expert_count = exp_size // 2
    capacity = min(row_count, 6 * token_count // (exp_size * exp_size))
    hit_expert, hit_slot = slot_tables(routes, expert_count, capacity)
    gate_local = w_gate[0]
    up_local = w_up[0]
    down_local = w_down[0]
    all_rows, all_routes = (
        lax.all_gather(normed[None], "ctx", axis=0, tiled=True),
        lax.all_gather(routes[None], "ctx", axis=0, tiled=True),
    )
    every_expert, every_slot = slot_tables(all_routes, expert_count, capacity)
    picker = jnp.repeat(jnp.einsum("crke,crks->cesr", every_expert, every_slot), 2, axis=1).astype(
        jnp.bfloat16
    )
    outgoing = jnp.einsum(
        "cosr,crd->cosd", picker, all_rows, preferred_element_type=jnp.float32
    ).astype(jnp.bfloat16)
    arrived = lax.all_to_all(outgoing, "exp", split_axis=1, concat_axis=1, tiled=True)
    gate_part = jnp.einsum("abcd,dh->abch", arrived, gate_local, preferred_element_type=jnp.float32)
    up_part = jnp.einsum("abcd,dh->abch", arrived, up_local, preferred_element_type=jnp.float32)
    hidden = (jax.nn.silu(gate_part) * up_part).astype(jnp.bfloat16)
    partial_out = jnp.einsum(
        "abch,hn->abcn",
        lax.all_gather(hidden, "ctx", axis=3, tiled=True),
        down_local,
        preferred_element_type=jnp.float32,
    )
    came_back = lax.all_to_all(
        lax.all_to_all(partial_out, "ctx", split_axis=0, concat_axis=3, tiled=True),
        "exp",
        split_axis=1,
        concat_axis=1,
        tiled=True,
    )
    halves = came_back[0].reshape(expert_count, 2, capacity, came_back.shape[-1])
    paired = halves[:, 0] + halves[:, 1]
    mixing = jnp.einsum("rk,rke,rks->res", route_weight, hit_expert, hit_slot)
    moe_sum = jnp.einsum("res,esd->rd", mixing, paired, precision=HIGHEST)
    return (resid.astype(jnp.float32) + moe_sum).astype(jnp.bfloat16)


MESH = pl.DeviceIdType.MESH
PROJ_TILES = 6
WIDE = 256


def dot32(left, right):
    return jnp.dot(left, right, preferred_element_type=jnp.float32)


def layer_kernel(
    zs,
    capacity,
    resid_in,
    queries,
    keys,
    values,
    out_gate,
    log_decay,
    attn_gain,
    out_proj_hbm,
    moe_gain,
    routes,
    route_weight,
    w_gate_hbm,
    w_up_hbm,
    w_down_hbm,
    mixed,
    out_proj,
    w_gate,
    w_up,
    w_rest,
    w_down,
    info,
    state_out,
    state_in,
    gated,
    pair_out,
    pair_in,
    proj_out,
    proj_in,
    resid,
    rows_in,
    picked,
    hidden_own,
    hidden_in,
    expert_sum,
    half_out,
    half_in,
    back_out,
    back_in,
    last_out,
    last_in,
    load_sem,
    info_send,
    info_recv,
    one_send,
    one_recv,
    pair_send,
    pair_recv,
    proj_send,
    proj_recv,
    gather_send,
    gather_recv,
    ctx_send,
    ctx_recv,
    core_send,
    core_recv,
    pass_send,
    pass_recv,
    hidden_send,
    hidden_recv,
    half_send,
    half_recv,
    back_send,
    back_recv,
):
    ctx = lax.axis_index("ctx")
    exp = lax.axis_index("exp")
    core = lax.rem(exp, 2)
    level = exp // 2
    row_count, width = resid_in.shape
    tokens = queries.shape[0]
    heads = log_decay.shape[0]
    head_width = queries.shape[1] // heads
    half = w_gate_hbm.shape[2]
    whole = half // WIDE * WIDE
    rest = half - whole
    columns = w_down_hbm.shape[2]
    cap_rows = zs * capacity
    tile = width // PROJ_TILES
    other_ctx = 1 - ctx

    def ahead(d):
        return lax.rem(level + d, zs)

    def behind(d):
        return lax.rem(level + zs - d, zs)

    def device(at_ctx, at_level, at_core):
        return {"ctx": at_ctx, "exp": at_level * 2 + at_core}

    core_partner = device(ctx, level, 1 - core)
    ctx_partner = device(other_ctx, level, core)

    loads = [
        pltpu.make_async_copy(out_proj_hbm, out_proj, load_sem.at[0]),
        pltpu.make_async_copy(w_gate_hbm.at[0, :, pl.ds(0, whole)], w_gate, load_sem.at[1]),
        pltpu.make_async_copy(w_up_hbm.at[0, :, pl.ds(0, whole)], w_up, load_sem.at[2]),
        pltpu.make_async_copy(
            w_gate_hbm.at[0, :, pl.ds(whole, rest)], w_rest.at[:, pl.ds(0, rest)], load_sem.at[3]
        ),
        pltpu.make_async_copy(
            w_up_hbm.at[0, :, pl.ds(whole, rest)], w_rest.at[:, pl.ds(rest, rest)], load_sem.at[4]
        ),
        pltpu.make_async_copy(w_down_hbm.at[0], w_down, load_sem.at[5]),
    ]
    for load in loads:
        load.start()

    barrier = pltpu.get_barrier_semaphore()
    peers = [core_partner, ctx_partner]
    for d in range(1, zs):
        peers.append(device(ctx, ahead(d), core))
        peers.append(device(other_ctx, ahead(d), core))
    for peer in peers:
        pl.semaphore_signal(barrier, inc=1, device_id=peer, device_id_type=MESH)

    def send(source, target, send_sem, recv_sem, peer):
        copy = pltpu.make_async_remote_copy(
            src_ref=source,
            dst_ref=target,
            send_sem=send_sem,
            recv_sem=recv_sem,
            device_id=peer,
            device_id_type=MESH,
        )
        copy.start()
        return copy

    sent = []
    lane = lax.broadcasted_iota(jnp.int32, (row_count, 128), 1)
    diagonal = lax.broadcasted_iota(jnp.int32, (row_count, row_count), 0) == lax.broadcasted_iota(
        jnp.int32, (row_count, row_count), 1
    )

    def upright_pair(flat):
        return [
            jnp.sum(jnp.where(diagonal, flat[k : k + 1, :], 0.0), axis=1, keepdims=True)
            for k in range(2)
        ]

    own_routes = upright_pair(routes[...].astype(jnp.float32))
    own_weight = upright_pair(route_weight[...])
    info[0, 0] = jnp.where(
        lane == 0,
        own_routes[0],
        jnp.where(lane == 1, own_routes[1], jnp.where(lane == 2, own_weight[0], own_weight[1])),
    )

    later_row = lax.broadcasted_iota(jnp.int32, (tokens, tokens), 0)
    later_col = lax.broadcasted_iota(jnp.int32, (tokens, tokens), 1)
    causal = later_row >= later_col
    sums = []
    for h in range(heads):
        span = pl.ds(h * head_width, head_width)
        spread = jnp.broadcast_to(log_decay[h : h + 1, :], (tokens, tokens))
        upright = jnp.transpose(spread)
        cum_col = jnp.sum(jnp.where(causal, spread, 0.0), axis=1, keepdims=True)
        cum_row = jnp.sum(jnp.where(later_row <= later_col, upright, 0.0), axis=0, keepdims=True)
        sums.append((cum_col, cum_row))
        tail = jnp.exp(cum_row[:, tokens - 1 : tokens] - cum_row)
        key_up = jnp.transpose(keys[:, span].astype(jnp.float32)) * tail
        state_out[h] = dot32(key_up.astype(jnp.bfloat16), values[:, span]).astype(jnp.bfloat16)

    pl.semaphore_wait(barrier, len(peers))
    state_copy = send(state_out, state_in, one_send.at[0], one_recv.at[0], ctx_partner)
    infos = []
    for rel in range(2):
        for d in range(zs):
            if rel or d:
                infos.append(
                    send(
                        info.at[0, 0],
                        info.at[rel, d],
                        info_send.at[rel * zs + d],
                        info_recv.at[rel * zs + d],
                        device(other_ctx if rel else ctx, ahead(d), core),
                    )
                )
    inner = []
    for h in range(heads):
        span = pl.ds(h * head_width, head_width)
        cum_col, cum_row = sums[h]
        scores = lax.dot_general(
            queries[:, span],
            keys[:, span],
            (((1,), (1,)), ((), ())),
            preferred_element_type=jnp.float32,
        )
        decay = jnp.where(causal, jnp.exp(jnp.minimum(cum_col - cum_row, 0.0)), 0.0)
        inner.append(dot32((scores * decay).astype(jnp.bfloat16), values[:, span]))
    state_copy.wait_recv()
    for h in range(heads):
        span = pl.ds(h * head_width, head_width)
        earlier = dot32(queries[:, span], state_in[h]) * jnp.exp(sums[h][0])
        attended = inner[h] + jnp.where(ctx == 0, 0.0, earlier)
        scale = lax.rsqrt(jnp.mean(attended * attended, axis=-1, keepdims=True) + 1e-06)
        opening = jax.nn.sigmoid(out_gate[:, span].astype(jnp.float32))
        gated[:, span] = (opening * attended * scale * attn_gain[:, span]).astype(jnp.bfloat16)

    order = [
        gated[pl.ds(pl.multiple_of(2 * row_count * ahead(d) + row_count * side, row_count), row_count), :]
        for side in (1 - core, core)
        for d in range(zs)
    ]
    ordered = jnp.concatenate(order, axis=0)
    loads[0].wait()
    split = zs * row_count
    pairs = []
    mine = []
    for n in range(PROJ_TILES):
        product = dot32(ordered, out_proj[:, n * tile : (n + 1) * tile])
        pair_out[n] = product[:split].astype(jnp.bfloat16)
        pairs.append(send(pair_out.at[n], pair_in.at[n], pair_send.at[n], pair_recv.at[n], core_partner))
        mine.append(product[split:])
    projected = []
    for n in range(PROJ_TILES):
        pairs[n].wait_recv()
        total = mine[n] + pair_in[n].astype(jnp.float32)
        for d in range(1, zs):
            proj_out[n, d] = total[d * row_count : (d + 1) * row_count].astype(jnp.bfloat16)
            projected.append(
                send(
                    proj_out.at[n, d],
                    proj_in.at[n, d],
                    proj_send.at[n * zs + d],
                    proj_recv.at[n * zs + d],
                    device(ctx, ahead(d), core),
                )
            )
        part = slice(n * tile, (n + 1) * tile)
        resid[:, part] = resid_in[:, part].astype(jnp.float32) + total[:row_count]

    for copy in infos:
        copy.wait_recv()
    block = row_count
    routed = info[...].reshape(2 * zs * block, 128)
    routed_up = jnp.transpose(routed)
    mark = level.astype(jnp.float32)
    count = 2 * zs * block
    place_row = lax.broadcasted_iota(jnp.int32, (count, count), 0)
    place_col = lax.broadcasted_iota(jnp.int32, (count, count), 1)
    same = place_row // block == place_col // block
    hit_col = jnp.where((routed[:, 0:1] == mark) | (routed[:, 1:2] == mark), 1.0, 0.0)
    hit_row = jnp.where((routed_up[0:1] == mark) | (routed_up[1:2] == mark), 1.0, 0.0)
    slot_row = jnp.sum(
        jnp.where(same & (place_row < place_col), hit_col, 0.0), axis=0, keepdims=True
    ).astype(jnp.int32)
    slot_col = jnp.sum(
        jnp.where(same & (place_col < place_row), hit_row, 0.0), axis=1, keepdims=True
    ).astype(jnp.int32)
    index_row = lax.broadcasted_iota(jnp.int32, (1, count), 1) // block * capacity + slot_row
    index_col = lax.broadcasted_iota(jnp.int32, (count, 1), 0) // block * capacity + slot_col
    reach_rows = lax.broadcasted_iota(jnp.int32, (cap_rows, count), 0)
    picker = jnp.where((reach_rows == index_row) & (hit_row > 0.5), 1.0, 0.0).astype(jnp.bfloat16)
    reach_cols = lax.broadcasted_iota(jnp.int32, (count, 2 * cap_rows), 1)
    placer = jnp.where((reach_cols == index_col) & (hit_col > 0.5), 1.0, 0.0).astype(jnp.bfloat16)

    for n in range(PROJ_TILES):
        part = slice(n * tile, (n + 1) * tile)
        for d in range(1, zs):
            projected[n * (zs - 1) + d - 1].wait_recv()
            resid[:, part] += proj_in[n, d].astype(jnp.float32)
    settled = resid[...].astype(jnp.bfloat16).astype(jnp.float32)
    resid[...] = settled
    scale = lax.rsqrt(jnp.mean(settled * settled, axis=-1, keepdims=True) + 1e-06)
    rows_in[0] = (settled * scale * moe_gain[...]).astype(jnp.bfloat16)

    def cut(n):
        return pl.ds(n * tile, tile)

    gathers = [
        [
            send(
                rows_in.at[0, :, cut(n)],
                rows_in.at[d, :, cut(n)],
                gather_send.at[n * zs + d],
                gather_recv.at[n * zs + d],
                device(ctx, ahead(d), core),
            )
            for d in range(1, zs)
        ]
        for n in range(PROJ_TILES)
    ]
    to_ctx, to_core, passed = [], [], []

    def pass_on(n):
        to_ctx[n].wait_recv()
        passed.append(
            send(
                picked.at[1, 0, :, cut(n)],
                picked.at[1, 1, :, cut(n)],
                pass_send.at[n],
                pass_recv.at[n],
                core_partner,
            )
        )

    for n in range(PROJ_TILES):
        for copy in gathers[n]:
            copy.wait_recv()
        landed = rows_in[:, :, n * tile : (n + 1) * tile].reshape(zs * block, tile)
        picked[0, 0, :, cut(n)] = dot32(picker[:, : zs * block], landed).astype(jnp.bfloat16)
        source = picked.at[0, 0, :, cut(n)]
        to_ctx.append(
            send(source, picked.at[1, 0, :, cut(n)], ctx_send.at[n], ctx_recv.at[n], ctx_partner)
        )
        to_core.append(
            send(source, picked.at[0, 1, :, cut(n)], core_send.at[n], core_recv.at[n], core_partner)
        )
    for n in range(PROJ_TILES - 1):
        pass_on(n)
    for copy in to_core:
        copy.wait_recv()

    def activate(gate_part, up_part):
        return (jax.nn.silu(gate_part) * up_part).astype(jnp.bfloat16)

    def hide(rel):
        def step(n, carry):
            span = pl.ds(pl.multiple_of(n * WIDE, WIDE), WIDE)
            rows = picked[rel].reshape(2 * cap_rows, width)
            hidden_own[rel, :, span] = activate(
                dot32(rows, w_gate[:, span]), dot32(rows, w_up[:, span])
            )
            return carry

        lax.fori_loop(0, whole // WIDE, step, 0)
        both = dot32(picked[rel].reshape(2 * cap_rows, width), w_rest[...])
        hidden_own[rel, :, whole:] = activate(both[:, :rest], both[:, rest:])
        return send(
            hidden_own.at[rel],
            hidden_in.at[1 - rel],
            hidden_send.at[rel],
            hidden_recv.at[1 - rel],
            ctx_partner,
        )

    def lower_own():
        def step(n, carry):
            span = pl.ds(pl.multiple_of(n * WIDE, WIDE), WIDE)
            expert_sum[:, :, span] = dot32(
                hidden_own[...].reshape(4 * cap_rows, half),
                w_down[pl.ds(pl.multiple_of(ctx * half, 128), half), span],
            ).reshape(2, 2 * cap_rows, WIDE)
            return carry

        lax.fori_loop(0, columns // WIDE, step, 0)

    def lower(rel):
        def step(n, carry):
            span = pl.ds(pl.multiple_of(n * WIDE, WIDE), WIDE)
            expert_sum[rel, :, span] += dot32(
                hidden_in[rel], w_down[pl.ds(pl.multiple_of(other_ctx * half, 128), half), span]
            )
            return carry

        lax.fori_loop(0, columns // WIDE, step, 0)

    for load in loads[1:5]:
        load.wait()
    hidden_near = hide(0)
    pass_on(PROJ_TILES - 1)
    for copy in passed:
        copy.wait_recv()
    hidden_far = hide(1)
    loads[5].wait()
    lower_own()

    def incoming_hidden(rel):
        return pltpu.make_async_remote_copy(
            src_ref=hidden_own.at[1 - rel],
            dst_ref=hidden_in.at[rel],
            send_sem=hidden_send.at[1 - rel],
            recv_sem=hidden_recv.at[rel],
            device_id=ctx_partner,
            device_id_type=MESH,
        )

    halves = [None, None]
    backs = {}
    for rel in (1, 0):
        incoming_hidden(rel).wait_recv()
        lower(rel)
        half_out[rel] = expert_sum[rel, cap_rows:, :].astype(jnp.bfloat16)
        halves[rel] = send(
            half_out.at[rel], half_in.at[rel], half_send.at[rel], half_recv.at[rel], core_partner
        )
        halves[rel].wait_recv()
        total = (expert_sum[rel, :cap_rows, :] + half_in[rel].astype(jnp.float32)).astype(jnp.bfloat16)
        chosen = placer[rel * zs * block : (rel + 1) * zs * block, rel * cap_rows : (rel + 1) * cap_rows]
        spread_rows = dot32(chosen, total).astype(jnp.bfloat16)
        back_in[rel, 0] = spread_rows[:block]
        for d in range(1, zs):
            back_out[rel, d] = spread_rows[d * block : (d + 1) * block]
            backs[rel, d] = send(
                back_out.at[rel, d],
                back_in.at[rel, d],
                back_send.at[rel * zs + d],
                back_recv.at[rel * zs + d],
                device(ctx, behind(d), core),
            )

    def mix(rel):
        table = info[rel, 0]
        total = jnp.zeros((block, columns), jnp.float32)
        for d in range(zs):
            if d:
                backs[rel, d].wait_recv()
            expert = ahead(d).astype(jnp.float32)
            weight = jnp.where(table[:, 0:1] == expert, table[:, 2:3], 0.0) + jnp.where(
                table[:, 1:2] == expert, table[:, 3:4], 0.0
            )
            total = total + weight * back_in[rel, d].astype(jnp.float32)
        return total

    last_out[...] = mix(1).astype(jnp.bfloat16)
    last = send(last_out, last_in, one_send.at[1], one_recv.at[1], ctx_partner)
    near = pl.ds(pl.multiple_of(ctx * columns, 128), columns)
    far = pl.ds(pl.multiple_of(other_ctx * columns, 128), columns)
    mixed[:, near] = (resid[:, near] + mix(0)).astype(jnp.bfloat16)
    last.wait_recv()
    mixed[:, far] = (resid[:, far] + last_in[...].astype(jnp.float32)).astype(jnp.bfloat16)

    sent += [state_copy, hidden_near, hidden_far, last] + to_ctx + to_core + passed
    sent += sum(gathers, [])
    for copy in sent + infos + pairs + projected + halves + list(backs.values()):
        copy.wait_send()


def per_device_kernel(
    resid_in,
    queries,
    keys,
    values,
    out_gate,
    log_decay,
    attn_gain,
    out_proj,
    moe_gain,
    routes,
    route_weight,
    w_gate,
    w_up,
    w_down,
):
    zs = lax.axis_size("exp") // 2
    row_count, width = resid_in.shape
    tokens = queries.shape[0]
    heads = log_decay.shape[0]
    head_width = queries.shape[1] // heads
    capacity = min(row_count, 6 * tokens // (4 * zs * zs))
    cap_rows = zs * capacity
    half = w_gate.shape[2]
    whole = half // WIDE * WIDE
    rest = half - whole
    columns = w_down.shape[2]
    tile = width // PROJ_TILES
    low = jnp.bfloat16
    dma = pltpu.SemaphoreType.DMA
    vmem = pl.BlockSpec(memory_space=pltpu.VMEM)
    away = pl.BlockSpec(memory_space=pl.ANY)
    return pl.pallas_call(
        functools.partial(layer_kernel, zs, capacity),
        out_shape=jax.ShapeDtypeStruct((row_count, width), low),
        in_specs=[vmem] * 7 + [away] + [vmem] * 3 + [away] * 3,
        out_specs=vmem,
        scratch_shapes=[
            pltpu.VMEM(out_proj.shape, low),
            pltpu.VMEM((width, whole), low),
            pltpu.VMEM((width, whole), low),
            pltpu.VMEM((width, 2 * rest), low),
            pltpu.VMEM(w_down.shape[1:], low),
            pltpu.VMEM((2, zs, row_count, 128), jnp.float32),
            pltpu.VMEM((heads, head_width, head_width), low),
            pltpu.VMEM((heads, head_width, head_width), low),
            pltpu.VMEM(queries.shape, low),
            pltpu.VMEM((PROJ_TILES, zs * row_count, tile), low),
            pltpu.VMEM((PROJ_TILES, zs * row_count, tile), low),
            pltpu.VMEM((PROJ_TILES, zs, row_count, tile), low),
            pltpu.VMEM((PROJ_TILES, zs, row_count, tile), low),
            pltpu.VMEM((row_count, width), jnp.float32),
            pltpu.VMEM((zs, row_count, width), low),
            pltpu.VMEM((2, 2, cap_rows, width), low),
            pltpu.VMEM((2, 2 * cap_rows, half), low),
            pltpu.VMEM((2, 2 * cap_rows, half), low),
            pltpu.VMEM((2, 2 * cap_rows, columns), jnp.float32),
            pltpu.VMEM((2, cap_rows, columns), low),
            pltpu.VMEM((2, cap_rows, columns), low),
            pltpu.VMEM((2, zs, row_count, columns), low),
            pltpu.VMEM((2, zs, row_count, columns), low),
            pltpu.VMEM((row_count, columns), low),
            pltpu.VMEM((row_count, columns), low),
            dma((6,)),
            dma((2 * zs,)),
            dma((2 * zs,)),
            dma((2,)),
            dma((2,)),
            dma((PROJ_TILES,)),
            dma((PROJ_TILES,)),
            dma((PROJ_TILES * zs,)),
            dma((PROJ_TILES * zs,)),
            dma((PROJ_TILES * zs,)),
            dma((PROJ_TILES * zs,)),
            dma((PROJ_TILES,)),
            dma((PROJ_TILES,)),
            dma((PROJ_TILES,)),
            dma((PROJ_TILES,)),
            dma((PROJ_TILES,)),
            dma((PROJ_TILES,)),
            dma((2,)),
            dma((2,)),
            dma((2,)),
            dma((2,)),
            dma((2 * zs,)),
            dma((2 * zs,)),
        ],
        compiler_params=pltpu.CompilerParams(
            collective_id=0, has_side_effects=True, vmem_limit_bytes=56 * 1024 * 1024
        ),
        cost_estimate=pl.CostEstimate(
            flops=12 * cap_rows * width * half * 2, bytes_accessed=6 * width * half, transcendentals=0
        ),
    )(
        resid_in,
        queries,
        keys,
        values,
        out_gate,
        log_decay,
        attn_gain.reshape(1, -1),
        out_proj,
        moe_gain.reshape(1, -1),
        routes.T,
        route_weight.T,
        w_gate,
        w_up,
        w_down,
    )


def solution(mesh):
    pairs_of_two = mesh.shape["ctx"] == 2 and mesh.shape["exp"] % 2 == 0
    return jax.shard_map(
        per_device_kernel if pairs_of_two else per_device,
        mesh=mesh,
        in_specs=(
            P(("groups", "ctx", "exp"), None),
            P(("groups", "ctx"), "exp"),
            P(("groups", "ctx"), "exp"),
            P(("groups", "ctx"), "exp"),
            P(("groups", "ctx"), "exp"),
            P("exp", ("groups", "ctx")),
            P("exp"),
            P("exp", None),
            P(),
            P(("groups", "ctx", "exp"), None),
            P(("groups", "ctx", "exp"), None),
            P("exp", None, "ctx"),
            P("exp", None, "ctx"),
            P("exp", None, "ctx"),
        ),
        out_specs=P(("groups", "ctx", "exp"), None),
        check_vma=False,
    )
```
